32 devices in a mesh: gx: 2 (over y), gy: 16 (over z, x, core).
Axes of the slice: x: 2, y: 2, z: 4, core: 2. Of those that a mesh axis runs over, the one named last changes fastest.
Arguments:
- source: float32 [64, 4096], P('gx', 'gy'), may hold values from -6 to 6
- potential: float32 [64, 4096], P('gx', 'gy'), may hold values from -1.5 to 1.5
- mobility_along: float32 [64, 4096], P('gx', 'gy'), may hold values from 0.3 to 3
- mobility_across: float32 [64, 4096], P('gx', 'gy'), may hold values from 0.3 to 3
- recombination: float32 [64, 4096], P('gx', 'gy'), may hold values from 0.002 to 0.05
- counts: int32 [2, 16], P('gx', 'gy'), may hold values from 8 to 32, as said below
- basis: float32 [64, 294912], P('gx', 'gy'), may hold values from -1 to 1
- coarse_inverse: float32 [1024, 1024], P(('gx', 'gy')), may hold values from -8 to 8
Outputs:
- solution: float32 [64, 4096], P('gx', 'gy')
- residual: float32 [64, 4096], P('gx', 'gy')
The draws below stay inside these ranges and needn't reach their ends.
Inputs may be any that keep to these rules, and one draw needn't show every extreme that they name: `counts`: the number of a subdomain's rows of basis that are in use.
All inputs are finite; a program needn't handle non-finite values.
Results may differ from the reference program's by a relative error of at most 0.003.
Values sent between devices are 32-bit elements; how exact they have to be, the bound alone decides.
A program may use at most 64 MiB of HBM per device.

```python
import math
import jax
import jax.numpy as jnp
from jax import lax

CX = 32
CY = 256
OV = 16
KMAX = 32
SWEEPS = 8
SUBX = 2
SUBY = 16
SUBS = 32
NX = 64
NY = 4096
PX = 64
PY = 288
EXTC = 18432
NC = 1024


def draw_counts(key, part):
    key = jax.random.fold_in(key, 11)
    values = jax.random.randint(key, (SUBX, SUBY), KMAX // 4, KMAX + 1)
    values = values.at[0, 0].set(KMAX)
    values = values.at[0, 1].set(KMAX // 4)
    return values.astype(jnp.int32)


def draw_basis(key, part):
    key = jax.random.fold_in(key, 31)
    keys = jax.random.split(key, 5)
    shape = (SUBX, KMAX, SUBY)
    freq_rows = jax.random.uniform(keys[0], shape, jnp.float32, 0.0, 3.0 * math.pi / PX)
    freq_cols = jax.random.uniform(keys[1], shape, jnp.float32, 0.0, 6.0 * math.pi / PY)
    phase_rows = jax.random.uniform(keys[2], shape, jnp.float32, -math.pi, math.pi)
    phase_cols = jax.random.uniform(keys[3], shape, jnp.float32, -math.pi, math.pi)
    row_coord = jnp.arange(PX, dtype=jnp.float32) + 0.5
    col_coord = jnp.arange(PY, dtype=jnp.float32) + 0.5
    wave_rows = jnp.cos(freq_rows[..., None] * row_coord + phase_rows[..., None])
    wave_cols = jnp.cos(freq_cols[..., None] * col_coord + phase_cols[..., None])
    smooth_part = wave_rows[..., :, None] * wave_cols[..., None, :]
    full_shape = (SUBX, KMAX, SUBY, PX, PY)
    rough_part = jnp.clip(jax.random.normal(keys[4], full_shape, jnp.float32), -4.0, 4.0)
    values = (2.0 * smooth_part + 0.25 * rough_part) / math.sqrt(EXTC)
    return values.reshape(SUBX * KMAX, SUBY * EXTC)


def draw_coarse_inverse(key, part):
    key = jax.random.fold_in(key, 23)
    noise_key, diagonal_key = jax.random.split(key)
    noise = jnp.clip(jax.random.normal(noise_key, (NC, NC), jnp.float32), -3.0, 3.0)
    diagonal_values = jnp.exp(jax.random.uniform(diagonal_key, (NC,), jnp.float32, math.log(2.0), math.log(8.0)))
    diagonal_values = jnp.where(jnp.arange(NC) == 0, 8.0, diagonal_values)
    row_index = lax.broadcasted_iota(jnp.int32, (NC, NC), 0)
    column_index = lax.broadcasted_iota(jnp.int32, (NC, NC), 1)
    row_sub = row_index // KMAX
    column_sub = column_index // KMAX
    distance = (jnp.abs(row_sub // SUBY - column_sub // SUBY) + jnp.abs(row_sub % SUBY - column_sub % SUBY)).astype(jnp.float32)
    scale = 1.5 * jnp.exp(-0.5 * distance) / math.sqrt(KMAX) + 4.0 / math.sqrt(NC)
    on_diagonal = row_index == column_index
    return jnp.where(on_diagonal, diagonal_values[:, None], noise * scale)


def block_levels(rng, dims, cuts, low, high):
    def one(position, blocks):
        heights = jax.random.uniform(jax.random.fold_in(jax.random.fold_in(rng, 6), position), (blocks,), jnp.float32, low / len(cuts), high / len(cuts))
        return jnp.repeat(jnp.exp(heights), dims[position] // blocks).reshape((-1,) + (1,) * (len(dims) - position - 1))

    factor_of = one(*cuts[0])
    for cut in cuts[1:]:
        factor_of = factor_of * one(*cut)
    return factor_of


def gaussian(stream_key, extent, width, most, pieces=(), kind=jnp.bfloat16):
    gain = block_levels(stream_key, extent, pieces, -0.22, 0.18) if pieces else 1.0
    values = jax.random.normal(stream_key, extent, jnp.float32) * width * gain
    return jnp.minimum(jnp.maximum(values, -most), most).astype(kind)


def setup_inputs(seed: int = 0) -> dict:
    key_of = jax.random.split(jax.random.key(seed), 9)
    source = gaussian(key_of[0], (NX, NY), 1.0, 6.0, ((0, 2), (1, 16)), jnp.float32)
    potential = jnp.clip(jax.random.uniform(key_of[1], (NX, NY), jnp.float32, -1.5, 1.5) * block_levels(key_of[1], (NX, NY), ((0, 2), (1, 16)), -0.4, 0.0), -1.5, 1.5)
    mobility_along = jnp.clip(jnp.exp(math.log(3.0) - 2.3025851 * jax.random.uniform(key_of[2], (NX, NY), jnp.float32) ** block_levels(key_of[2], (NX, NY), ((0, 2), (1, 16)), -0.2, 0.2)), 0.3, 3.0)
    mobility_across = jnp.clip(jnp.exp(math.log(3.0) - 2.3025851 * jax.random.uniform(key_of[3], (NX, NY), jnp.float32) ** block_levels(key_of[3], (NX, NY), ((0, 2), (1, 16)), -0.2, 0.2)), 0.3, 3.0)
    recombination = jnp.clip(jnp.exp(math.log(0.05) - 3.218876 * jax.random.uniform(key_of[4], (NX, NY), jnp.float32) ** block_levels(key_of[4], (NX, NY), ((0, 2), (1, 16)), -0.2, 0.2)), 0.002, 0.05)
    counts = draw_counts(jax.random.fold_in(key_of[8], 71), 0)
    basis = draw_basis(jax.random.fold_in(key_of[8], 71), 0)
    coarse_inverse = draw_coarse_inverse(jax.random.fold_in(key_of[8], 71), 0)
    return dict(source=source, potential=potential, mobility_along=mobility_along, mobility_across=mobility_across, recombination=recombination, counts=counts, basis=basis, coarse_inverse=coarse_inverse)


OMEGA = 0.8
EPSILON = 1e-06
HIGHEST_PRECISION = lax.Precision.HIGHEST

def face_weights(potential, mobility_along, mobility_across):
    along_first = jnp.sqrt(mobility_along[:-1, :] * mobility_along[1:, :])
    along_second = jnp.sqrt(mobility_across[:, :-1] * mobility_across[:, 1:])
    rise_first = potential[1:, :] - potential[:-1, :]
    rise_second = potential[:, 1:] - potential[:, :-1]
    downward = along_first * jnp.exp(0.5 * rise_first)
    upward = along_first * jnp.exp(-0.5 * rise_first)
    eastward = along_second * jnp.exp(0.5 * rise_second)
    westward = along_second * jnp.exp(-0.5 * rise_second)
    return (downward, upward, eastward, westward)

def build(potential, mobility_along, mobility_across, recombination):
    downward, upward, eastward, westward = face_weights(potential, mobility_along, mobility_across)
    diagonal = recombination + jnp.pad(upward, ((0, 1), (0, 0))) + jnp.pad(downward, ((1, 0), (0, 0)))
    diagonal = diagonal + jnp.pad(westward, ((0, 0), (0, 1))) + jnp.pad(eastward, ((0, 0), (1, 0)))
    return (diagonal, (downward, upward, eastward, westward))

def coupled(field, faces):
    downward, upward, eastward, westward = faces
    total = jnp.pad(downward * field[1:, :], ((0, 1), (0, 0)))
    total = total + jnp.pad(upward * field[:-1, :], ((1, 0), (0, 0)))
    total = total + jnp.pad(eastward * field[:, 1:], ((0, 0), (0, 1)))
    total = total + jnp.pad(westward * field[:, :-1], ((0, 0), (1, 0)))
    return total

def smooth(vector_patch, diagonal, faces):
    field = jnp.zeros_like(vector_patch)
    for sweep in range(SWEEPS):
        field = field + OMEGA * (vector_patch - (diagonal * field - coupled(field, faces))) / diagonal
    return field

def least_squares(source_norm, first_first, second_first, first_second, second_second, third_second):
    radius = jnp.sqrt(first_first * first_first + second_first * second_first)
    cosine = first_first / radius
    sine = second_first / radius
    upper_right = cosine * first_second + sine * second_second
    lower_right = cosine * second_second - sine * first_second
    radius_two = jnp.sqrt(lower_right * lower_right + third_second * third_second)
    weight_two = lower_right / radius_two * (-sine * source_norm) / radius_two
    weight_one = (cosine * source_norm - upper_right * weight_two) / radius
    remainder_one = source_norm - first_first * weight_one - first_second * weight_two
    remainder_two = -second_first * weight_one - second_second * weight_two
    remainder_three = -third_second * weight_two
    return (weight_one, weight_two, remainder_one, remainder_two, remainder_three)

def fold(parts):
    middle = parts[:, :, OV:-OV, :]
    from_above = jnp.pad(parts[:-1, :, -OV:, :], ((1, 0), (0, 0), (0, 0), (0, 0)))
    from_below = jnp.pad(parts[1:, :, :OV, :], ((0, 1), (0, 0), (0, 0), (0, 0)))
    middle = middle.at[:, :, :OV, :].add(from_above)
    middle = middle.at[:, :, -OV:, :].add(from_below)
    inner = middle[:, :, :, OV:-OV]
    from_left = jnp.pad(middle[:, :-1, :, -OV:], ((0, 0), (1, 0), (0, 0), (0, 0)))
    from_right = jnp.pad(middle[:, 1:, :, :OV], ((0, 0), (0, 1), (0, 0), (0, 0)))
    inner = inner.at[:, :, :, :OV].add(from_left)
    inner = inner.at[:, :, :, -OV:].add(from_right)
    return inner

def reference(source, potential, mobility_along, mobility_across, recombination, counts, basis, coarse_inverse):
    grid_diagonal, grid_faces = build(potential, mobility_along, mobility_across, recombination)

    def apply(field):
        return grid_diagonal * field - coupled(field, grid_faces)
    padded_fields = [jnp.pad(array, OV) for array in (potential, mobility_along, mobility_across, recombination)]
    live_all = (lax.broadcasted_iota(jnp.int32, (SUBX, SUBY, KMAX), 2) < counts[:, :, None]).astype(jnp.float32)
    live_all = live_all.reshape(SUBS, KMAX)
    indices = jnp.arange(SUBS, dtype=jnp.int32)

    def corner_of(index):
        row_block = (index // SUBY).astype(jnp.int32)
        column_block = (index % SUBY).astype(jnp.int32)
        return (row_block, column_block)

    def precondition(vector):
        padded = jnp.pad(vector, OV)

        def local(index):
            row_block, column_block = corner_of(index)
            start = (row_block * CX, column_block * CY)
            fields = [lax.dynamic_slice(array, start, (PX, PY)) for array in padded_fields]
            diagonal, faces = build(fields[0], fields[1], fields[2], fields[3])
            row_place = row_block * CX - OV + lax.broadcasted_iota(jnp.int32, (PX, PY), 0)
            column_place = column_block * CY - OV + lax.broadcasted_iota(jnp.int32, (PX, PY), 1)
            inside = ((row_place >= 0) & (row_place < NX) & (column_place >= 0) & (column_place < NY)).astype(jnp.float32)
            diagonal = diagonal + (1.0 - inside)
            vector_patch = lax.dynamic_slice(padded, start, (PX, PY))
            solved = smooth(vector_patch, diagonal, faces)[OV:OV + CX, OV:OV + CY]
            block = lax.dynamic_slice(basis, (row_block * KMAX, column_block * EXTC), (KMAX, EXTC))
            restricted = jnp.dot(block, vector_patch.reshape(EXTC), precision=HIGHEST_PRECISION)
            return (solved, restricted)
        solved, restricted = lax.map(local, indices)
        restricted = restricted * live_all
        coarse = jnp.dot(coarse_inverse, restricted.reshape(NC), precision=HIGHEST_PRECISION)
        coarse = coarse.reshape(SUBS, KMAX) * live_all

        def spread(items):
            index, weights = items
            row_block, column_block = corner_of(index)
            block = lax.dynamic_slice(basis, (row_block * KMAX, column_block * EXTC), (KMAX, EXTC))
            return jnp.dot(weights, block, precision=HIGHEST_PRECISION).reshape(PX, PY)
        parts = lax.map(spread, (indices, coarse))
        folded = fold(parts.reshape(SUBX, SUBY, PX, PY))
        total = solved.reshape(SUBX, SUBY, CX, CY) + folded
        return total.transpose(0, 2, 1, 3).reshape(NX, NY)
    source_norm = jnp.sqrt(jnp.sum(source * source) + EPSILON)
    first = source / source_norm
    first_dir = precondition(first)
    image = apply(first_dir)
    first_first = jnp.sum(first * image)
    image = image - first_first * first
    second_first = jnp.sqrt(jnp.sum(image * image) + EPSILON)
    second = image / second_first
    second_dir = precondition(second)
    image = apply(second_dir)
    first_second = jnp.sum(first * image)
    second_second = jnp.sum(second * image)
    image = image - first_second * first - second_second * second
    third_second = jnp.sqrt(jnp.sum(image * image) + EPSILON)
    third = image / third_second
    weight_one, weight_two, remainder_one, remainder_two, remainder_three = least_squares(source_norm, first_first, second_first, first_second, second_second, third_second)
    solution = weight_one * first_dir + weight_two * second_dir
    residual = remainder_one * first + remainder_two * second + remainder_three * third
    return (solution, residual)
```

```python
import functools
import math
import jax
import jax.numpy as jnp
from jax import lax
from jax.experimental import pallas as pl
from jax.experimental.pallas import tpu as pltpu
from jax.sharding import PartitionSpec as P

OV = 16
SWEEPS = 8
OMEGA = 0.8
EPSILON = 1e-06
LANES = 128
ROWS = 24
SIDE = 64
MESH = pl.DeviceIdType.MESH

NEAR = [(i, j) for i in (-1, 0, 1) for j in (-1, 0, 1) if (i, j) != (0, 0)]
FAR = [(i, j) for i in (-2, 2) for j in (-1, 0, 1)]


def least_squares(
    source_norm, first_first, second_first, first_second, second_second, third_second
):
    radius = jnp.sqrt(first_first * first_first + second_first * second_first)
    cosine = first_first / radius
    sine = second_first / radius
    upper_right = cosine * first_second + sine * second_second
    lower_right = cosine * second_second - sine * first_second
    radius_two = jnp.sqrt(lower_right * lower_right + third_second * third_second)
    weight_two = lower_right / radius_two * (-sine * source_norm) / radius_two
    weight_one = (cosine * source_norm - upper_right * weight_two) / radius
    remainder_one = source_norm - first_first * weight_one - first_second * weight_two
    remainder_two = -second_first * weight_one - second_second * weight_two
    remainder_three = -third_second * weight_two
    return (weight_one, weight_two, remainder_one, remainder_two, remainder_three)


def part_slices(di, dj, height, breadth):
    high, wide = height + 2 * ROWS, breadth + 2 * SIDE
    margin = ROWS - OV
    if di == 0:
        start, size, to = margin, height + 2 * OV, margin
    elif di == 1:
        start, size = height, ROWS + OV
        to = 0
    elif di == -1:
        size = ROWS + OV
        start, to = margin, high - size
    elif di == 2:
        start, size, to = 2 * height, margin, 0
    else:
        start, size, to = margin, margin, high - margin
    if dj == 0:
        lane, width, lane_to = 0, wide, 0
    elif dj == 1:
        lane, width, lane_to = wide - LANES, LANES, 0
    else:
        lane, width, lane_to = 0, LANES, wide - LANES
    return (pl.ds(start, size), pl.ds(lane, width), pl.ds(to, size), pl.ds(lane_to, width))


def kernel(
    gx, gy, far,
    counts, source, potential, along, across, recombination, basis_hbm, inverse_hbm,
    solution_out, residual_out,
    basis, inverse, grown, fields, pack_out, pack_in, part, total, flat, row_out, gathered,
    *rest,
):
    directions = NEAR + far
    arrived = rest[: len(directions)]
    load_sem, send_sem, recv_sem, row_send, row_recv = rest[len(directions):]
    devices = gx * gy
    x = lax.axis_index("gx")
    y = lax.axis_index("gy")
    me = x * gy + y
    height, breadth = source.shape
    vectors = basis.shape[0]
    high, wide = height + 2 * ROWS, breadth + 2 * SIDE
    px, py = height + 2 * OV, breadth + 2 * OV
    group = LANES // math.gcd(py, LANES)
    lines, length = px // group, py * group
    own_rows = pl.ds(ROWS, height)

    load_basis = pltpu.make_async_copy(basis_hbm, basis, load_sem.at[0])
    load_inverse = pltpu.make_async_copy(inverse_hbm, inverse, load_sem.at[1])
    load_basis.start()
    load_inverse.start()

    grown[...] = jnp.zeros_like(grown)
    fields[...] = jnp.zeros_like(fields)
    pack_in[...] = jnp.zeros_like(pack_in)
    for ref in arrived:
        ref[...] = jnp.zeros_like(ref)

    barrier = pltpu.get_barrier_semaphore()

    def greet(step, carry):
        other = lax.rem(me + step, devices)
        pl.semaphore_signal(
            barrier, inc=1, device_id=(other // gy, lax.rem(other, gy)), device_id_type=MESH
        )
        return carry

    lax.fori_loop(1, devices, greet, 0)

    grown[own_rows, pl.ds(LANES, breadth)] = source[...]
    own_fields = [potential[...], jnp.sqrt(along[...]), jnp.sqrt(across[...]), recombination[...]]
    lane = lax.broadcasted_iota(jnp.int32, (height, LANES), 1)
    strip = LANES // 4
    to_east = jnp.zeros((height, LANES), jnp.float32)
    to_west = jnp.zeros((height, LANES), jnp.float32)
    for f in range(4):
        fields[f, own_rows, :] = own_fields[f]
        here = (lane >= f * strip) & (lane < (f + 1) * strip)
        east = pltpu.roll(own_fields[f][:, breadth - LANES:], ((f + 1) * strip) % LANES, 1)
        west = pltpu.roll(own_fields[f][:, :LANES], f * strip, 1)
        to_east = jnp.where(here, east, to_east)
        to_west = jnp.where(here, west, to_west)
    pack_out[0] = to_east
    pack_out[1] = to_west

    pl.semaphore_wait(barrier, devices - 1)

    def present(di, dj):
        return (x + di >= 0) & (x + di < gx) & (y + dj >= 0) & (y + dj < gy)

    def copy(src, dst, phase, number, di, dj):
        return pltpu.make_async_remote_copy(
            src_ref=src,
            dst_ref=dst,
            send_sem=send_sem.at[phase, number],
            recv_sem=recv_sem.at[phase, number],
            device_id=(x + di, y + dj),
            device_id_type=MESH,
        )

    def source_copy(number, di, dj):
        start, size, to = {0: (0, height, ROWS), 1: (height - OV, OV, ROWS - OV), -1: (0, OV, ROWS + height)}[di]
        column, width, column_to = {
            0: (0, breadth, LANES),
            1: (breadth - LANES, LANES, 0),
            -1: (0, LANES, LANES + breadth),
        }[dj]
        return copy(
            grown.at[pl.ds(ROWS + start, size), pl.ds(LANES + column, width)],
            grown.at[pl.ds(to, size), pl.ds(column_to, width)],
            0, number, di, dj,
        )

    def field_copy(number, di, dj):
        start, size, to = {0: (0, height, ROWS), 1: (height - ROWS, ROWS, 0), -1: (0, ROWS, ROWS + height)}[di]
        if dj == 0:
            src = fields.at[:, pl.ds(ROWS + start, size), :]
            dst = fields.at[:, pl.ds(to, size), :]
        else:
            side = 0 if dj == 1 else 1
            src = pack_out.at[side, pl.ds(start, size), :]
            dst = pack_in.at[side, pl.ds(to, size), :]
        return copy(src, dst, 1, number, di, dj)

    def part_copy(turn):
        def make(number, di, dj):
            rows, columns, _, _ = part_slices(di, dj, height, breadth)
            return copy(
                part.at[turn, rows, columns], arrived[number].at[turn], 2 + turn, number, di, dj
            )

        return make

    def start_all(make, chosen):
        for number, (di, dj) in enumerate(chosen):
            @pl.when(present(di, dj))
            def _(number=number, di=di, dj=dj):
                make(number, di, dj).start()

    def receive_all(make, chosen):
        for number, (di, dj) in enumerate(chosen):
            @pl.when(present(-di, -dj))
            def _(number=number, di=di, dj=dj):
                make(number, di, dj).wait_recv()

    def sent_all(make, chosen):
        for number, (di, dj) in enumerate(chosen):
            @pl.when(present(di, dj))
            def _(number=number, di=di, dj=dj):
                make(number, di, dj).wait_send()

    def share(turn):
        def send(step, carry):
            other = lax.rem(me + step, devices)
            pltpu.make_async_remote_copy(
                src_ref=row_out.at[turn],
                dst_ref=gathered.at[turn, me],
                send_sem=row_send.at[turn],
                recv_sem=row_recv.at[turn],
                device_id=(other // gy, lax.rem(other, gy)),
                device_id_type=MESH,
            ).start()
            return carry

        gathered[turn, me] = row_out[turn]
        lax.fori_loop(1, devices, send, 0)

    def row_bytes(turn, sem):
        some = gathered.at[turn, pl.ds(0, devices - 1)]
        return pltpu.make_async_copy(some, some, sem.at[turn])

    def collect(turn):
        row_bytes(turn, row_recv).wait()
        return gathered[turn].reshape(devices, LANES)

    start_all(source_copy, NEAR)
    start_all(field_copy, NEAR)

    frame_row = lax.broadcasted_iota(jnp.int32, (high, wide), 0)
    frame_lane = lax.broadcasted_iota(jnp.int32, (high, wide), 1)
    grid_row = frame_row - ROWS + x * height
    grid_lane = frame_lane - SIDE + y * breadth
    inside = (
        (grid_row >= 0) & (grid_row < height * gx) & (grid_lane >= 0) & (grid_lane < breadth * gy)
    )
    own = (
        (frame_row >= ROWS) & (frame_row < ROWS + height)
        & (frame_lane >= SIDE) & (frame_lane < SIDE + breadth)
    )
    line_lane = lax.broadcasted_iota(jnp.int32, (lines, wide), 1)
    in_patch = (line_lane >= SIDE - OV) & (line_lane < SIDE + breadth + OV)
    vector_index = lax.broadcasted_iota(jnp.int32, (vectors, 1), 0)
    live = (vector_index < counts[0, 0]).astype(jnp.float32)
    quarter = lax.rem(me, 4)
    row_lane = lax.broadcasted_iota(jnp.int32, (1, LANES), 1)
    spot = (
        lax.broadcasted_iota(jnp.int32, (vectors, LANES), 1)
        == lax.broadcasted_iota(jnp.int32, (vectors, LANES), 0) + strip * quarter
    )
    device_row = lax.broadcasted_iota(jnp.int32, (devices, LANES), 0)
    device_lane = lax.broadcasted_iota(jnp.int32, (devices, LANES), 1)
    is_coarse = device_lane // strip == lax.rem(device_row, 4)

    def restrict():
        pieces = None
        for q in range(group):
            taken = jnp.concatenate(
                [
                    total[t, pl.ds(ROWS - OV + q, lines, stride=group), :]
                    for t in range(wide // LANES)
                ],
                axis=1,
            )
            taken = jnp.where(in_patch, taken, 0.0)
            taken = jnp.concatenate(
                [taken, jnp.zeros((lines, length - wide), jnp.float32)], axis=1
            )
            taken = pltpu.roll(taken, (py * q - (SIDE - OV)) % length, 1)
            pieces = taken if pieces is None else pieces + taken
        flat[...] = pieces
        summed = jnp.zeros((vectors, length), jnp.float32)
        for a in range(lines):
            summed = summed + basis[:, a * length:(a + 1) * length] * flat[a:a + 1, :]
        folded = summed[:, :LANES]
        for t in range(1, length // LANES):
            folded = folded + summed[:, t * LANES:(t + 1) * LANES]
        coarse = jnp.sum(folded, axis=1, keepdims=True) * live
        return jnp.sum(jnp.where(spot, coarse, 0.0), axis=0, keepdims=True)

    def spread(rows):
        rows = jnp.where(is_coarse, rows, 0.0)
        joined = rows
        for i in range(1, 4):
            joined = joined + pltpu.roll(rows, i, 0)
        summed = jnp.zeros((vectors, LANES), jnp.float32)
        for b in range(devices // 4):
            summed = (
                summed + inverse[:, b * LANES:(b + 1) * LANES] * joined[4 * b + 3:4 * b + 4, :]
            )
        weights = jnp.sum(summed, axis=1, keepdims=True) * live
        weights = jnp.broadcast_to(weights, (vectors, LANES))
        weights = jnp.concatenate([weights] * (length // LANES), axis=1)
        for a in range(lines):
            flat[a:a + 1, :] = jnp.sum(
                basis[:, a * length:(a + 1) * length] * weights, axis=0, keepdims=True
            )
        whole = flat[...]
        for t in range(wide // LANES):
            total[t] = jnp.zeros((high, LANES), jnp.float32)
        for q in range(group):
            moved = pltpu.roll(whole, (SIDE - OV - py * q) % length, 1)[:, :wide]
            moved = jnp.where(in_patch, moved, 0.0)
            for t in range(wide // LANES):
                total[t, pl.ds(ROWS - OV + q, lines, stride=group), :] = (
                    moved[:, t * LANES:(t + 1) * LANES]
                )
        return get_total()

    def set_total(value):
        for t in range(wide // LANES):
            total[t] = value[:, t * LANES:(t + 1) * LANES]

    def get_total():
        return jnp.concatenate([total[t] for t in range(wide // LANES)], axis=1)

    def around(value):
        return (
            pltpu.roll(value, high - 1, 0),
            pltpu.roll(value, 1, 0),
            pltpu.roll(value, wide - 1, 1),
            pltpu.roll(value, 1, 1),
        )

    def exchange(turn, value):
        part[turn] = value
        start_all(part_copy(turn), directions)
        receive_all(part_copy(turn), directions)
        set_total(value)
        for number, (di, dj) in enumerate(directions):
            _, _, rows, columns = part_slices(di, dj, height, breadth)
            got = arrived[number][turn]
            first = columns.start // LANES
            for t in range(columns.size // LANES):
                total[first + t, rows, :] = (
                    total[first + t, rows, :] + got[:, t * LANES:(t + 1) * LANES]
                )
        return jnp.where(inside, get_total(), 0.0)

    def dots(pairs):
        row = jnp.zeros((1, LANES), jnp.float32)
        place = lax.rem(quarter + 1, 4) * strip
        for i, (one, other) in enumerate(pairs):
            product = jnp.sum(jnp.where(own, one * other, 0.0), axis=0, keepdims=True)
            value = jnp.sum(product, axis=1, keepdims=True)
            row = jnp.where(row_lane == place + i, value, row)
        return row

    def whole_sums(rows, count):
        others = jnp.where(is_coarse, 0.0, rows)
        row = jnp.sum(others, axis=0, keepdims=True)
        return [
            jnp.sum(jnp.where(lax.rem(row_lane, strip) == i, row, 0.0), axis=1, keepdims=True)
            for i in range(count)
        ]

    receive_all(source_copy, NEAR)
    first_vector = pltpu.roll(grown[...], wide + LANES - SIDE, 1)[:, :wide]
    set_total(first_vector)
    load_basis.wait()
    row_out[0] = restrict()
    share(0)

    receive_all(field_copy, NEAR)
    patch = []
    side_lane = lax.broadcasted_iota(jnp.int32, (high, LANES), 1)
    for f in range(4):
        base = jnp.concatenate([fields[f], jnp.zeros((high, LANES), jnp.float32)], axis=1)
        base = pltpu.roll(base, SIDE, 1)
        west = pltpu.roll(pack_in[0], (SIDE - (f + 1) * strip) % LANES, 1)
        east = pltpu.roll(pack_in[1], (SIDE - f * strip) % LANES, 1)
        left = jnp.where((side_lane >= SIDE - strip) & (side_lane < SIDE), west, base[:, :LANES])
        right = jnp.where(
            (side_lane >= SIDE) & (side_lane < SIDE + strip), east, base[:, wide - LANES:]
        )
        patch.append(jnp.concatenate([left, base[:, LANES:wide - LANES], right], axis=1))
    level = jnp.exp(0.5 * patch[0])
    level_inverse = jnp.exp(-0.5 * patch[0])
    root_along, root_across = patch[1], patch[2]
    faces = (
        root_along * pltpu.roll(root_along, high - 1, 0),
        root_along * pltpu.roll(root_along, 1, 0),
        root_across * pltpu.roll(root_across, wide - 1, 1),
        root_across * pltpu.roll(root_across, 1, 1),
    )
    outflow = jnp.zeros((high, wide), jnp.float32)
    for face, beside in zip(faces, around(level_inverse)):
        outflow = outflow + face * beside
    diagonal = patch[3] + level * outflow
    diagonal = jnp.where(diagonal > 0.0, diagonal, 1.0)
    step_size = OMEGA / diagonal
    step_faces = [face * step_size for face in faces]
    step_level = step_size * level

    def smooth(vector):
        scaled = step_level * vector
        field = scaled
        for sweep in range(SWEEPS - 1):
            moved = (1.0 - OMEGA) * field + scaled
            for face, beside in zip(step_faces, around(field)):
                moved = moved + face * beside
            field = moved
        return jnp.where(own, level_inverse * field, 0.0)

    def apply(vector):
        scaled = level * vector
        image = diagonal * scaled
        for face, beside in zip(faces, around(scaled)):
            image = image - face * beside
        return level_inverse * image

    solved = smooth(first_vector)
    load_inverse.wait()
    first_dir = exchange(0, solved + spread(collect(0)))
    image = apply(first_dir)

    set_total(image)
    row_out[1] = restrict() + dots(
        [(first_vector, first_vector), (first_vector, image), (image, image)]
    )
    share(1)
    solved = smooth(image)
    rows = collect(1)
    second_dir = exchange(1, solved + spread(rows))
    squares, mixed, image_squares = whole_sums(rows, 3)
    source_norm = jnp.sqrt(squares + EPSILON)
    shrink = 1.0 / source_norm
    first_first = mixed * shrink * shrink
    left_over = (
        image_squares * shrink * shrink
        - 2.0 * first_first * first_first
        + first_first * first_first * (squares * shrink * shrink)
    )
    second_first = jnp.sqrt(jnp.maximum(left_over, 0.0) + EPSILON)
    first = first_vector * shrink
    first_dir = first_dir * shrink
    second = (image * shrink - first_first * first) / second_first
    second_dir = (second_dir * shrink - first_first * first_dir) / second_first
    image = apply(second_dir)
    row_out[2] = dots(
        [(first, image), (second, image), (image, image), (first, first), (second, second),
         (first, second)]
    )
    share(2)
    first_second, second_second, image_squares, ones, twos, cross = whole_sums(collect(2), 6)
    left_over = (
        image_squares
        - 2.0 * (first_second * first_second + second_second * second_second)
        + first_second * first_second * ones
        + second_second * second_second * twos
        + 2.0 * first_second * second_second * cross
    )
    third_second = jnp.sqrt(jnp.maximum(left_over, 0.0) + EPSILON)
    image = image - first_second * first - second_second * second
    weight_one, weight_two, remainder_one, remainder_two, remainder_three = least_squares(
        source_norm, first_first, second_first, first_second, second_second, third_second
    )
    answer = weight_one * first_dir + weight_two * second_dir
    remainder = (
        remainder_one * first + remainder_two * second + (remainder_three / third_second) * image
    )
    solution_out[...] = pltpu.roll(answer[ROWS:ROWS + height], wide - SIDE, 1)[:, :breadth]
    residual_out[...] = pltpu.roll(remainder[ROWS:ROWS + height], wide - SIDE, 1)[:, :breadth]

    sent_all(source_copy, NEAR)
    sent_all(field_copy, NEAR)
    for turn in range(2):
        sent_all(part_copy(turn), directions)
    for turn in range(3):
        row_bytes(turn, row_send).wait()


def on_device(
    gx, gy,
    source, potential, mobility_along, mobility_across, recombination, counts, basis, coarse_inverse
):
    height, breadth = source.shape
    vectors = basis.shape[0]
    devices = gx * gy
    high, wide = height + 2 * ROWS, breadth + 2 * SIDE
    px, py = height + 2 * OV, breadth + 2 * OV
    group = LANES // math.gcd(py, LANES)
    far = FAR if gx > 2 else []
    arrived = []
    for di, dj in NEAR + far:
        rows, columns, _, _ = part_slices(di, dj, height, breadth)
        arrived.append(pltpu.VMEM((2, rows.size, columns.size), jnp.float32))
    vmem = pl.BlockSpec(memory_space=pltpu.VMEM)
    hbm = pl.BlockSpec(memory_space=pl.ANY)
    ways = len(arrived)
    return pl.pallas_call(
        functools.partial(kernel, gx, gy, far),
        out_shape=(
            jax.ShapeDtypeStruct((height, breadth), jnp.float32),
            jax.ShapeDtypeStruct((height, breadth), jnp.float32),
        ),
        in_specs=[pl.BlockSpec(memory_space=pltpu.SMEM)] + [vmem] * 5 + [hbm] * 2,
        out_specs=(vmem, vmem),
        scratch_shapes=[
            pltpu.VMEM(basis.shape, jnp.float32),
            pltpu.VMEM(coarse_inverse.shape, jnp.float32),
            pltpu.VMEM((high, breadth + 2 * LANES), jnp.float32),
            pltpu.VMEM((4, high, breadth), jnp.float32),
            pltpu.VMEM((2, height, LANES), jnp.float32),
            pltpu.VMEM((2, high, LANES), jnp.float32),
            pltpu.VMEM((2, high, wide), jnp.float32),
            pltpu.VMEM((wide // LANES, high, LANES), jnp.float32),
            pltpu.VMEM((px // group, py * group), jnp.float32),
            pltpu.VMEM((3, 1, LANES), jnp.float32),
            pltpu.VMEM((3, devices, 1, LANES), jnp.float32),
            *arrived,
            pltpu.SemaphoreType.DMA((2,)),
            pltpu.SemaphoreType.DMA((4, ways)),
            pltpu.SemaphoreType.DMA((4, ways)),
            pltpu.SemaphoreType.DMA((3,)),
            pltpu.SemaphoreType.DMA((3,)),
        ],
        compiler_params=pltpu.CompilerParams(
            collective_id=0, has_side_effects=True, vmem_limit_bytes=32 * 1024 * 1024
        ),
    )(counts, source, potential, mobility_along, mobility_across, recombination, basis, coarse_inverse)


def solution(mesh):
    placed = (P("gx", "gy"),) * 7 + (P(("gx", "gy"), None),)
    return jax.shard_map(
        functools.partial(on_device, mesh.shape["gx"], mesh.shape["gy"]),
        mesh=mesh,
        in_specs=placed,
        out_specs=(P("gx", "gy"), P("gx", "gy")),
        check_vma=False,
    )
```

```python
import functools
import math
import jax
import jax.numpy as jnp
from jax import lax
from jax.experimental import pallas as pl
from jax.experimental.pallas import tpu as pltpu
from jax.sharding import PartitionSpec as P

OV = 16
SWEEPS = 8
OMEGA = 0.8
EPSILON = 1e-06
LANES = 128
ROWS = 24
SIDE = 64
NARROW = 8
MESH = pl.DeviceIdType.MESH

NEAR = [(i, j) for i in (-1, 0, 1) for j in (-1, 0, 1) if (i, j) != (0, 0)]
FAR = [(i, j) for i in (-2, 2) for j in (-1, 0, 1)]


def least_squares(
    source_norm, first_first, second_first, first_second, second_second, third_second
):
    radius = jnp.sqrt(first_first * first_first + second_first * second_first)
    cosine = first_first / radius
    sine = second_first / radius
    upper_right = cosine * first_second + sine * second_second
    lower_right = cosine * second_second - sine * first_second
    radius_two = jnp.sqrt(lower_right * lower_right + third_second * third_second)
    weight_two = lower_right / radius_two * (-sine * source_norm) / radius_two
    weight_one = (cosine * source_norm - upper_right * weight_two) / radius
    remainder_one = source_norm - first_first * weight_one - first_second * weight_two
    remainder_two = -second_first * weight_one - second_second * weight_two
    remainder_three = -third_second * weight_two
    return (weight_one, weight_two, remainder_one, remainder_two, remainder_three)


def part_slices(turn, di, dj, height, breadth):
    high, wide = height + 2 * ROWS, breadth + 2 * SIDE
    margin = ROWS - OV
    reach = ROWS if turn == 0 else NARROW
    if di == 0:
        used = min(reach, OV)
        start, size, to = ROWS - used, height + 2 * used, ROWS - used
    elif di == 1:
        start, size, to = height + ROWS - reach, reach + OV, ROWS - reach
    elif di == -1:
        start, size, to = margin, reach + OV, ROWS + height - OV
    elif di == 2:
        start, size, to = 2 * height, margin, 0
    else:
        start, size, to = margin, margin, high - margin
    if dj == 0:
        lane, width, lane_to = 0, wide, 0
    elif dj == 1:
        lane, width, lane_to = wide - LANES, LANES, 0
    else:
        lane, width, lane_to = 0, LANES, wide - LANES
    return (pl.ds(start, size), pl.ds(lane, width), pl.ds(to, size), pl.ds(lane_to, width))


def kernel(
    gx, gy, far,
    counts_hbm, source, potential, along, across, recombination, basis_hbm, inverse_hbm,
    solution_out, residual_out,
    counts, basis, inverse, grown, raw, fields, pack_out, pack_in, part, total, flat, row_out,
    gathered, *rest,
):
    directions = (NEAR + far, NEAR)
    arrived = (rest[: len(directions[0])], rest[len(directions[0]):][: len(NEAR)])
    load_sem, send_sem, recv_sem, row_send, row_recv = rest[len(directions[0]) + len(NEAR):]
    devices = gx * gy
    x = lax.axis_index("gx")
    y = lax.axis_index("gy")
    me = x * gy + y
    height, breadth = source.shape
    vectors = basis.shape[0]
    high, wide = height + 2 * ROWS, breadth + 2 * SIDE
    px, py = height + 2 * OV, breadth + 2 * OV
    group = LANES // math.gcd(py, LANES)
    lines, length = px // group, py * group
    own_rows = pl.ds(ROWS, height)

    def wrapped(place, step, size):
        return jnp.where(place + step >= size, place + step - size, place + step)

    few = devices <= 64
    along_x = [wrapped(x, a, gx) if a else x for a in range(gx)]
    along_y = [wrapped(y, b, gy) if b else y for b in range(gy)] if few else []

    def to_others(act):
        for a in range(gx):
            if few:
                for b in range(gy):
                    if a or b:
                        act((along_x[a], along_y[b]))
            else:
                def step(b, carry, a=a):
                    act((along_x[a], wrapped(y, b, gy)))
                    return carry

                lax.fori_loop(0 if a else 1, gy, step, 0)

    sources = [
        (source, grown.at[own_rows, pl.ds(LANES, breadth)]),
        (potential, fields.at[0, own_rows, :]),
        (along, raw.at[0]),
        (across, raw.at[1]),
        (recombination, fields.at[3, own_rows, :]),
        (counts_hbm, counts),
        (inverse_hbm, inverse),
        (basis_hbm, basis),
    ]
    loads = [
        pltpu.make_async_copy(src, dst, load_sem.at[i]) for i, (src, dst) in enumerate(sources)
    ]
    for load in loads:
        load.start()
    barrier = pltpu.get_barrier_semaphore()
    to_others(
        lambda place: pl.semaphore_signal(barrier, inc=1, device_id=place, device_id_type=MESH)
    )

    def present(di, dj):
        return (x + di >= 0) & (x + di < gx) & (y + dj >= 0) & (y + dj < gy)

    def copy(src, dst, phase, number, di, dj):
        return pltpu.make_async_remote_copy(
            src_ref=src,
            dst_ref=dst,
            send_sem=send_sem.at[phase, number],
            recv_sem=recv_sem.at[phase, number],
            device_id=(x + di, y + dj),
            device_id_type=MESH,
        )

    def source_target(di, dj):
        start, size, to = {
            0: (0, height, ROWS),
            1: (height - OV, OV, ROWS - OV),
            -1: (0, OV, ROWS + height),
        }[di]
        column, width, column_to = {
            0: (0, breadth, LANES),
            1: (breadth - LANES, LANES, 0),
            -1: (0, LANES, LANES + breadth),
        }[dj]
        return (
            grown.at[pl.ds(ROWS + start, size), pl.ds(LANES + column, width)],
            grown.at[pl.ds(to, size), pl.ds(column_to, width)],
        )

    def field_target(di, dj):
        start, size, to = {
            0: (0, height, ROWS),
            1: (height - ROWS, ROWS, 0),
            -1: (0, ROWS, ROWS + height),
        }[di]
        if dj == 0:
            return (
                fields.at[:, pl.ds(ROWS + start, size), :], fields.at[:, pl.ds(to, size), :]
            )
        side = 0 if dj == 1 else 1
        return (pack_out.at[side, pl.ds(start, size), :], pack_in.at[side, pl.ds(to, size), :])

    def source_copy(number, di, dj):
        return copy(*source_target(di, dj), 0, number, di, dj)

    def field_copy(number, di, dj):
        return copy(*field_target(di, dj), 1, number, di, dj)

    def part_copy(turn):
        def make(number, di, dj):
            rows, columns, _, _ = part_slices(turn, di, dj, height, breadth)
            return copy(
                part.at[turn, rows, columns], arrived[turn][number], 2 + turn, number, di, dj
            )

        return make

    def start_all(make, chosen):
        for number, (di, dj) in enumerate(chosen):
            @pl.when(present(di, dj))
            def _(number=number, di=di, dj=dj):
                make(number, di, dj).start()

    def receive_all(make, chosen):
        for number, (di, dj) in enumerate(chosen):
            @pl.when(present(-di, -dj))
            def _(number=number, di=di, dj=dj):
                make(number, di, dj).wait_recv()

    def sent_all(make, chosen):
        for number, (di, dj) in enumerate(chosen):
            @pl.when(present(di, dj))
            def _(number=number, di=di, dj=dj):
                make(number, di, dj).wait_send()

    def share(turn):
        gathered[turn, me] = row_out[turn]
        to_others(
            lambda place: pltpu.make_async_remote_copy(
                src_ref=row_out.at[turn],
                dst_ref=gathered.at[turn, me],
                send_sem=row_send.at[turn],
                recv_sem=row_recv.at[turn],
                device_id=place,
                device_id_type=MESH,
            ).start()
        )

    def row_bytes(turn, sem):
        some = gathered.at[turn, pl.ds(0, devices - 1)]
        return pltpu.make_async_copy(some, some, sem.at[turn])

    def collect(turn):
        row_bytes(turn, row_recv).wait()
        return gathered[turn].reshape(devices, LANES)

    for number, (di, dj) in enumerate(directions[0]):
        @pl.when(jnp.logical_not(present(-di, -dj)))
        def _(number=number, di=di, dj=dj):
            targets = [arrived[0][number]]
            if (di, dj) in NEAR:
                targets += [
                    arrived[1][number], source_target(di, dj)[1], field_target(di, dj)[1]
                ]
            for target in targets:
                target[...] = jnp.zeros(target.shape, jnp.float32)

    unused = jnp.zeros((ROWS - OV, breadth + 2 * LANES), jnp.float32)
    grown[: ROWS - OV, :] = unused
    grown[high - ROWS + OV:, :] = unused

    loads[0].wait()
    pl.semaphore_wait(barrier, devices - 1)
    start_all(source_copy, NEAR)

    for load in loads[1:5]:
        load.wait()
    fields[1, own_rows, :] = jnp.sqrt(raw[0])
    fields[2, own_rows, :] = jnp.sqrt(raw[1])
    lane = lax.broadcasted_iota(jnp.int32, (height, LANES), 1)
    strip = LANES // 4
    to_east = jnp.zeros((height, LANES), jnp.float32)
    to_west = jnp.zeros((height, LANES), jnp.float32)
    for f in range(4):
        here = (lane >= f * strip) & (lane < (f + 1) * strip)
        east = fields[f, own_rows, breadth - LANES:]
        west = fields[f, own_rows, :LANES]
        to_east = jnp.where(here, pltpu.roll(east, ((f + 1) * strip) % LANES, 1), to_east)
        to_west = jnp.where(here, pltpu.roll(west, f * strip, 1), to_west)
    pack_out[0] = to_east
    pack_out[1] = to_west
    start_all(field_copy, NEAR)
    loads[5].wait()

    frame_row = lax.broadcasted_iota(jnp.int32, (high, wide), 0)
    frame_lane = lax.broadcasted_iota(jnp.int32, (high, wide), 1)
    grid_row = frame_row - ROWS + x * height
    grid_lane = frame_lane - SIDE + y * breadth
    inside = (
        (grid_row >= 0) & (grid_row < height * gx) & (grid_lane >= 0) & (grid_lane < breadth * gy)
    )
    own_lane = lax.broadcasted_iota(jnp.int32, (height, wide), 1)
    own = (own_lane >= SIDE) & (own_lane < SIDE + breadth)
    line_lane = lax.broadcasted_iota(jnp.int32, (lines, wide), 1)
    in_patch = (line_lane >= SIDE - OV) & (line_lane < SIDE + breadth + OV)
    vector_index = lax.broadcasted_iota(jnp.int32, (vectors, 1), 0)
    live = (vector_index < counts[0, 0]).astype(jnp.float32)
    quarter = lax.rem(me, 4)
    row_lane = lax.broadcasted_iota(jnp.int32, (1, LANES), 1)
    spot = (
        lax.broadcasted_iota(jnp.int32, (vectors, LANES), 1)
        == lax.broadcasted_iota(jnp.int32, (vectors, LANES), 0) + strip * quarter
    )
    device_row = lax.broadcasted_iota(jnp.int32, (devices, LANES), 0)
    device_lane = lax.broadcasted_iota(jnp.int32, (devices, LANES), 1)
    is_coarse = device_lane // strip == lax.rem(device_row, 4)

    def restrict():
        pieces = None
        for q in range(group):
            taken = jnp.concatenate(
                [
                    total[t, pl.ds(ROWS - OV + q, lines, stride=group), :]
                    for t in range(wide // LANES)
                ],
                axis=1,
            )
            taken = jnp.where(in_patch, taken, 0.0)
            taken = jnp.concatenate(
                [taken, jnp.zeros((lines, length - wide), jnp.float32)], axis=1
            )
            taken = pltpu.roll(taken, (py * q - (SIDE - OV)) % length, 1)
            pieces = taken if pieces is None else pieces + taken
        flat[...] = pieces
        summed = jnp.zeros((vectors, length), jnp.float32)
        for a in range(lines):
            summed = summed + basis[:, a * length:(a + 1) * length] * flat[a:a + 1, :]
        folded = summed[:, :LANES]
        for t in range(1, length // LANES):
            folded = folded + summed[:, t * LANES:(t + 1) * LANES]
        coarse = jnp.sum(folded, axis=1, keepdims=True) * live
        return jnp.sum(jnp.where(spot, coarse, 0.0), axis=0, keepdims=True)

    def spread(rows):
        rows = jnp.where(is_coarse, rows, 0.0)
        joined = rows
        for i in range(1, 4):
            joined = joined + pltpu.roll(rows, i, 0)
        summed = jnp.zeros((vectors, LANES), jnp.float32)
        for b in range(devices // 4):
            summed = (
                summed + inverse[:, b * LANES:(b + 1) * LANES] * joined[4 * b + 3:4 * b + 4, :]
            )
        weights = jnp.sum(summed, axis=1, keepdims=True) * live
        weights = jnp.broadcast_to(weights, (vectors, LANES))
        weights = jnp.concatenate([weights] * (length // LANES), axis=1)
        for a in range(lines):
            flat[a:a + 1, :] = jnp.sum(
                basis[:, a * length:(a + 1) * length] * weights, axis=0, keepdims=True
            )
        whole = flat[...]
        for t in range(wide // LANES):
            total[t] = jnp.zeros((high, LANES), jnp.float32)
        for q in range(group):
            moved = pltpu.roll(whole, (SIDE - OV - py * q) % length, 1)[:, :wide]
            moved = jnp.where(in_patch, moved, 0.0)
            for t in range(wide // LANES):
                total[t, pl.ds(ROWS - OV + q, lines, stride=group), :] = (
                    moved[:, t * LANES:(t + 1) * LANES]
                )
        return get_total()

    def set_total(value):
        for t in range(wide // LANES):
            total[t] = value[:, t * LANES:(t + 1) * LANES]

    def get_total():
        return jnp.concatenate([total[t] for t in range(wide // LANES)], axis=1)

    def around(value):
        rows = value.shape[0]
        return (
            pltpu.roll(value, rows - 1, 0),
            pltpu.roll(value, 1, 0),
            pltpu.roll(value, wide - 1, 1),
            pltpu.roll(value, 1, 1),
        )

    def exchange(turn):
        start_all(part_copy(turn), directions[turn])
        set_total(part[turn])
        receive_all(part_copy(turn), directions[turn])
        for number, (di, dj) in enumerate(directions[turn]):
            _, _, rows, columns = part_slices(turn, di, dj, height, breadth)
            got = arrived[turn][number][...]
            first = columns.start // LANES
            for t in range(columns.size // LANES):
                total[first + t, rows, :] = (
                    total[first + t, rows, :] + got[:, t * LANES:(t + 1) * LANES]
                )
        return jnp.where(inside, get_total(), 0.0)

    def dots(pairs):
        row = jnp.zeros((1, LANES), jnp.float32)
        place = lax.rem(quarter + 1, 4) * strip
        for i, (one, other) in enumerate(pairs):
            product = jnp.sum(jnp.where(own, one * other, 0.0), axis=0, keepdims=True)
            value = jnp.sum(product, axis=1, keepdims=True)
            row = jnp.where(row_lane == place + i, value, row)
        return row

    def whole_sums(rows, count):
        others = jnp.where(is_coarse, 0.0, rows)
        row = jnp.sum(others, axis=0, keepdims=True)
        return [
            jnp.sum(jnp.where(lax.rem(row_lane, strip) == i, row, 0.0), axis=1, keepdims=True)
            for i in range(count)
        ]

    receive_all(source_copy, NEAR)
    first_vector = pltpu.roll(grown[...], wide + LANES - SIDE, 1)[:, :wide]
    set_total(first_vector)
    loads[7].wait()
    row_out[0] = restrict()
    share(0)

    receive_all(field_copy, NEAR)
    patch = []
    side_lane = lax.broadcasted_iota(jnp.int32, (high, LANES), 1)
    for f in range(4):
        base = jnp.concatenate([fields[f], jnp.zeros((high, LANES), jnp.float32)], axis=1)
        base = pltpu.roll(base, SIDE, 1)
        west = pltpu.roll(pack_in[0], (SIDE - (f + 1) * strip) % LANES, 1)
        east = pltpu.roll(pack_in[1], (SIDE - f * strip) % LANES, 1)
        left = jnp.where((side_lane >= SIDE - strip) & (side_lane < SIDE), west, base[:, :LANES])
        right = jnp.where(
            (side_lane >= SIDE) & (side_lane < SIDE + strip), east, base[:, wide - LANES:]
        )
        patch.append(jnp.concatenate([left, base[:, LANES:wide - LANES], right], axis=1))
    level = jnp.exp(0.5 * patch[0])
    level_inverse = jnp.exp(-0.5 * patch[0])
    root_along, root_across = patch[1], patch[2]
    faces = (
        root_along * pltpu.roll(root_along, high - 1, 0),
        root_along * pltpu.roll(root_along, 1, 0),
        root_across * pltpu.roll(root_across, wide - 1, 1),
        root_across * pltpu.roll(root_across, 1, 1),
    )
    outflow = jnp.zeros((high, wide), jnp.float32)
    for face, beside in zip(faces, around(level_inverse)):
        outflow = outflow + face * beside
    diagonal = patch[3] + level * outflow
    diagonal = jnp.where(diagonal > 0.0, diagonal, 1.0)
    near = slice(ROWS - NARROW, ROWS + height + NARROW)
    middle = slice(NARROW, NARROW + height)
    mine = slice(ROWS, ROWS + height)
    step_size = OMEGA / diagonal[near]
    step_faces = [face[near] * step_size for face in faces]
    step_level = step_size * level[near]
    own_level_inverse = level_inverse[mine]

    def smooth(vector):
        scaled = step_level * vector[near]
        field = scaled
        for sweep in range(SWEEPS - 1):
            moved = (1.0 - OMEGA) * field + scaled
            for face, beside in zip(step_faces, around(field)):
                moved = moved + face * beside
            field = moved
        return jnp.where(own, own_level_inverse * field[middle], 0.0)

    def apply(vector, rows):
        scaled = level[rows] * vector
        image = diagonal[rows] * scaled
        for face, beside in zip(faces, around(scaled)):
            image = image - face[rows] * beside
        return level_inverse[rows] * image

    def put_part(turn, solved, spreads):
        part[turn] = spreads
        part[turn, own_rows, :] = spreads[mine] + solved

    solved = smooth(first_vector)
    loads[6].wait()
    put_part(0, solved, spread(collect(0)))
    first_dir = exchange(0)
    image = apply(first_dir, slice(0, high))

    set_total(image)
    first_vector_own, image_own = first_vector[mine], image[mine]
    row_out[1] = restrict() + dots(
        [
            (first_vector_own, first_vector_own),
            (first_vector_own, image_own),
            (image_own, image_own),
        ]
    )
    share(1)
    solved = smooth(image)
    rows = collect(1)
    put_part(1, solved, spread(rows))
    second_dir = exchange(1)[near]
    first_dir, first_vector, image = first_dir[near], first_vector[near], image[near]
    squares, mixed, image_squares = whole_sums(rows, 3)
    source_norm = jnp.sqrt(squares + EPSILON)
    shrink = 1.0 / source_norm
    first_first = mixed * shrink * shrink
    left_over = (
        image_squares * shrink * shrink
        - 2.0 * first_first * first_first
        + first_first * first_first * (squares * shrink * shrink)
    )
    second_first = jnp.sqrt(jnp.maximum(left_over, 0.0) + EPSILON)
    first = first_vector * shrink
    first_dir = first_dir * shrink
    second = (image * shrink - first_first * first) / second_first
    second_dir = (second_dir * shrink - first_first * first_dir) / second_first
    image = apply(second_dir, near)[middle]
    first_dir, second_dir = first_dir[middle], second_dir[middle]
    first, second = first[middle], second[middle]
    row_out[2] = dots(
        [(first, image), (second, image), (image, image), (first, first), (second, second),
         (first, second)]
    )
    share(2)
    first_second, second_second, image_squares, ones, twos, cross = whole_sums(collect(2), 6)
    left_over = (
        image_squares
        - 2.0 * (first_second * first_second + second_second * second_second)
        + first_second * first_second * ones
        + second_second * second_second * twos
        + 2.0 * first_second * second_second * cross
    )
    third_second = jnp.sqrt(jnp.maximum(left_over, 0.0) + EPSILON)
    image = image - first_second * first - second_second * second
    weight_one, weight_two, remainder_one, remainder_two, remainder_three = least_squares(
        source_norm, first_first, second_first, first_second, second_second, third_second
    )
    answer = weight_one * first_dir + weight_two * second_dir
    remainder = (
        remainder_one * first + remainder_two * second + (remainder_three / third_second) * image
    )
    solution_out[...] = pltpu.roll(answer, wide - SIDE, 1)[:, :breadth]
    residual_out[...] = pltpu.roll(remainder, wide - SIDE, 1)[:, :breadth]

    sent_all(source_copy, NEAR)
    sent_all(field_copy, NEAR)
    for turn in range(2):
        sent_all(part_copy(turn), directions[turn])
    for turn in range(3):
        row_bytes(turn, row_send).wait()


def on_device(
    gx, gy,
    source, potential, mobility_along, mobility_across, recombination, counts, basis, coarse_inverse
):
    height, breadth = source.shape
    vectors = basis.shape[0]
    devices = gx * gy
    high, wide = height + 2 * ROWS, breadth + 2 * SIDE
    px, py = height + 2 * OV, breadth + 2 * OV
    group = LANES // math.gcd(py, LANES)
    far = FAR if gx > 2 else []
    arrived = []
    for turn, chosen in enumerate((NEAR + far, NEAR)):
        for di, dj in chosen:
            rows, columns, _, _ = part_slices(turn, di, dj, height, breadth)
            arrived.append(pltpu.VMEM((rows.size, columns.size), jnp.float32))
    vmem = pl.BlockSpec(memory_space=pltpu.VMEM)
    hbm = pl.BlockSpec(memory_space=pltpu.HBM)
    ways = len(NEAR + far)
    return pl.pallas_call(
        functools.partial(kernel, gx, gy, far),
        out_shape=(
            jax.ShapeDtypeStruct((height, breadth), jnp.float32),
            jax.ShapeDtypeStruct((height, breadth), jnp.float32),
        ),
        in_specs=[hbm] * 8,
        out_specs=(vmem, vmem),
        scratch_shapes=[
            pltpu.SMEM((1, 1), jnp.int32),
            pltpu.VMEM(basis.shape, jnp.float32),
            pltpu.VMEM(coarse_inverse.shape, jnp.float32),
            pltpu.VMEM((high, breadth + 2 * LANES), jnp.float32),
            pltpu.VMEM((2, height, breadth), jnp.float32),
            pltpu.VMEM((4, high, breadth), jnp.float32),
            pltpu.VMEM((2, height, LANES), jnp.float32),
            pltpu.VMEM((2, high, LANES), jnp.float32),
            pltpu.VMEM((2, high, wide), jnp.float32),
            pltpu.VMEM((wide // LANES, high, LANES), jnp.float32),
            pltpu.VMEM((px // group, py * group), jnp.float32),
            pltpu.VMEM((3, 1, LANES), jnp.float32),
            pltpu.VMEM((3, devices, 1, LANES), jnp.float32),
            *arrived,
            pltpu.SemaphoreType.DMA((8,)),
            pltpu.SemaphoreType.DMA((4, ways)),
            pltpu.SemaphoreType.DMA((4, ways)),
            pltpu.SemaphoreType.DMA((3,)),
            pltpu.SemaphoreType.DMA((3,)),
        ],
        compiler_params=pltpu.CompilerParams(
            collective_id=0, has_side_effects=True, vmem_limit_bytes=32 * 1024 * 1024
        ),
    )(counts, source, potential, mobility_along, mobility_across, recombination, basis, coarse_inverse)


def solution(mesh):
    placed = (P("gx", "gy"),) * 7 + (P(("gx", "gy"), None),)
    return jax.shard_map(
        functools.partial(on_device, mesh.shape["gx"], mesh.shape["gy"]),
        mesh=mesh,
        in_specs=placed,
        out_specs=(P("gx", "gy"), P("gx", "gy")),
        check_vma=False,
    )
```

```python
import functools
import math
import jax
import jax.numpy as jnp
from jax import lax
from jax.experimental import pallas as pl
from jax.experimental.pallas import tpu as pltpu
from jax.sharding import PartitionSpec as P

OV = 16
SWEEPS = 8
OMEGA = 0.8
EPSILON = 1e-06
LANES = 128
ROWS = 24
SIDE = 64
NARROW = 8
VMEM_GRANT = 63 * 1024 * 1024
MESH = pl.DeviceIdType.MESH

NEAR = [(i, j) for i in (-1, 0, 1) for j in (-1, 0, 1) if (i, j) != (0, 0)]
FAR = [(i, j) for i in (-2, 2) for j in (-1, 0, 1)]


def least_squares(
    source_norm, first_first, second_first, first_second, second_second, third_second
):
    radius = jnp.sqrt(first_first * first_first + second_first * second_first)
    cosine = first_first / radius
    sine = second_first / radius
    upper_right = cosine * first_second + sine * second_second
    lower_right = cosine * second_second - sine * first_second
    radius_two = jnp.sqrt(lower_right * lower_right + third_second * third_second)
    weight_two = lower_right / radius_two * (-sine * source_norm) / radius_two
    weight_one = (cosine * source_norm - upper_right * weight_two) / radius
    remainder_one = source_norm - first_first * weight_one - first_second * weight_two
    remainder_two = -second_first * weight_one - second_second * weight_two
    remainder_three = -third_second * weight_two
    return (weight_one, weight_two, remainder_one, remainder_two, remainder_three)


def split(gy):
    inner = 4
    while 4 * inner * inner <= gy:
        inner *= 2
    return inner


def part_slices(turn, di, dj, height, breadth):
    high, wide = height + 2 * ROWS, breadth + 2 * SIDE
    margin = ROWS - OV
    reach = ROWS if turn == 0 else NARROW
    if di == 0:
        used = min(reach, OV)
        start, size, to = ROWS - used, height + 2 * used, ROWS - used
    elif di == 1:
        start, size, to = height + ROWS - reach, reach + OV, ROWS - reach
    elif di == -1:
        start, size, to = margin, reach + OV, ROWS + height - OV
    elif di == 2:
        start, size, to = 2 * height, margin, 0
    else:
        start, size, to = margin, margin, high - margin
    if dj == 0:
        lane, width, lane_to = 0, wide, 0
    elif dj == 1:
        lane, width, lane_to = wide - LANES, LANES, 0
    else:
        lane, width, lane_to = 0, LANES, wide - LANES
    return (pl.ds(start, size), pl.ds(lane, width), pl.ds(to, size), pl.ds(lane_to, width))


def kernel(
    gx, gy, far,
    counts_hbm, source, potential, along, across, recombination, basis_hbm, inverse_hbm,
    solution_out, residual_out,
    counts, basis, inverse, grown, raw, fields, pack_out, pack_in, part, total, flat, row_out,
    gathered, *rest,
):
    directions = (NEAR + far, NEAR)
    arrived = (rest[: len(directions[0])], rest[len(directions[0]):][: len(NEAR)])
    load_sem, send_sem, recv_sem, row_send, row_recv, block_send, block_recv = rest[len(directions[0]) + len(NEAR):]
    devices = gx * gy
    x = lax.axis_index("gx")
    y = lax.axis_index("gy")
    height, breadth = source.shape
    vectors = basis.shape[0]
    high, wide = height + 2 * ROWS, breadth + 2 * SIDE
    px, py = height + 2 * OV, breadth + 2 * OV
    group = LANES // math.gcd(py, LANES)
    lines, length = px // group, py * group
    own_rows = pl.ds(ROWS, height)

    inner = split(gy)
    outer = gy // inner
    members = gx * inner
    which, seat = y // inner, lax.rem(y, inner)

    def wrapped(place, step, size):
        return jnp.where(place + step >= size, place + step - size, place + step) if step else place

    group_places = [
        (wrapped(x, a, gx), which * inner + wrapped(seat, b, inner))
        for a in range(gx) for b in range(inner) if a or b
    ]
    peer_places = [(x, wrapped(which, o, outer) * inner + seat) for o in range(1, outer)]
    slot = which * members + x * inner + seat

    def present(di, dj):
        return (x + di >= 0) & (x + di < gx) & (y + dj >= 0) & (y + dj < gy)

    def beyond(di, dj):
        return present(di, dj) & (seat == (inner - 1 if dj == 1 else 0))

    sources = [
        (source, grown.at[own_rows, pl.ds(LANES, breadth)]),
        (potential, fields.at[0, own_rows, :]),
        (along, raw.at[0]),
        (across, raw.at[1]),
        (recombination, fields.at[3, own_rows, :]),
        (counts_hbm, counts),
        (inverse_hbm, inverse),
        (basis_hbm, basis),
    ]
    loads = [
        pltpu.make_async_copy(src, dst, load_sem.at[i]) for i, (src, dst) in enumerate(sources)
    ]
    for load in loads:
        load.start()
    barrier = pltpu.get_barrier_semaphore()
    for place in group_places + peer_places:
        pl.semaphore_signal(barrier, inc=1, device_id=place, device_id_type=MESH)
    greeted = len(group_places) + len(peer_places)
    for di, dj in directions[0]:
        if dj != 0:
            greeted = greeted + jnp.where(beyond(di, dj), 1, 0)

            @pl.when(beyond(di, dj))
            def _(di=di, dj=dj):
                pl.semaphore_signal(
                    barrier, inc=1, device_id=(x + di, y + dj), device_id_type=MESH
                )

    def copy(src, dst, phase, number, di, dj):
        return pltpu.make_async_remote_copy(
            src_ref=src,
            dst_ref=dst,
            send_sem=send_sem.at[phase, number],
            recv_sem=recv_sem.at[phase, number],
            device_id=(x + di, y + dj),
            device_id_type=MESH,
        )

    def source_target(di, dj):
        start, size, to = {
            0: (0, height, ROWS),
            1: (height - OV, OV, ROWS - OV),
            -1: (0, OV, ROWS + height),
        }[di]
        column, width, column_to = {
            0: (0, breadth, LANES),
            1: (breadth - LANES, LANES, 0),
            -1: (0, LANES, LANES + breadth),
        }[dj]
        return (
            grown.at[pl.ds(ROWS + start, size), pl.ds(LANES + column, width)],
            grown.at[pl.ds(to, size), pl.ds(column_to, width)],
        )

    def field_target(di, dj):
        start, size, to = {
            0: (0, height, ROWS),
            1: (height - ROWS, ROWS, 0),
            -1: (0, ROWS, ROWS + height),
        }[di]
        if dj == 0:
            return (
                fields.at[:, pl.ds(ROWS + start, size), :], fields.at[:, pl.ds(to, size), :]
            )
        side = 0 if dj == 1 else 1
        return (pack_out.at[side, pl.ds(start, size), :], pack_in.at[side, pl.ds(to, size), :])

    def source_copy(number, di, dj):
        return copy(*source_target(di, dj), 0, number, di, dj)

    def field_copy(number, di, dj):
        return copy(*field_target(di, dj), 1, number, di, dj)

    def part_copy(turn):
        def make(number, di, dj):
            rows, columns, _, _ = part_slices(turn, di, dj, height, breadth)
            return copy(
                part.at[turn, rows, columns], arrived[turn][number], 2 + turn, number, di, dj
            )

        return make

    def start_all(make, chosen):
        for number, (di, dj) in enumerate(chosen):
            @pl.when(present(di, dj))
            def _(number=number, di=di, dj=dj):
                make(number, di, dj).start()

    def receive_all(make, chosen):
        for number, (di, dj) in enumerate(chosen):
            @pl.when(present(-di, -dj))
            def _(number=number, di=di, dj=dj):
                make(number, di, dj).wait_recv()

    def sent_all(make, chosen):
        for number, (di, dj) in enumerate(chosen):
            @pl.when(present(di, dj))
            def _(number=number, di=di, dj=dj):
                make(number, di, dj).wait_send()

    def share(turn):
        gathered[turn, slot] = row_out[turn]
        for place in group_places:
            pltpu.make_async_remote_copy(
                src_ref=row_out.at[turn],
                dst_ref=gathered.at[turn, slot],
                send_sem=row_send.at[turn],
                recv_sem=row_recv.at[turn],
                device_id=place,
                device_id_type=MESH,
            ).start()

    def row_bytes(turn, count, sem):
        some = gathered.at[turn, pl.ds(0, count)]
        return pltpu.make_async_copy(some, some, sem.at[turn])

    def pass_on(turn):
        row_bytes(turn, members - 1, row_recv).wait()
        rows = gathered.at[turn, pl.ds(which * members, members)]
        for place in peer_places:
            pltpu.make_async_remote_copy(
                src_ref=rows,
                dst_ref=rows,
                send_sem=block_send.at[turn],
                recv_sem=block_recv.at[turn],
                device_id=place,
                device_id_type=MESH,
            ).start()

    def collect(turn):
        row_bytes(turn, devices - members, block_recv).wait()
        return gathered[turn].reshape(devices, LANES)

    for number, (di, dj) in enumerate(directions[0]):
        @pl.when(jnp.logical_not(present(-di, -dj)))
        def _(number=number, di=di, dj=dj):
            targets = [arrived[0][number]]
            if (di, dj) in NEAR:
                targets += [
                    arrived[1][number], source_target(di, dj)[1], field_target(di, dj)[1]
                ]
            for target in targets:
                target[...] = jnp.zeros(target.shape, jnp.float32)

    unused = jnp.zeros((ROWS - OV, breadth + 2 * LANES), jnp.float32)
    grown[: ROWS - OV, :] = unused
    grown[high - ROWS + OV:, :] = unused

    loads[0].wait()
    pl.semaphore_wait(barrier, greeted)
    start_all(source_copy, NEAR)

    for load in loads[1:5]:
        load.wait()
    fields[1, own_rows, :] = jnp.sqrt(raw[0])
    fields[2, own_rows, :] = jnp.sqrt(raw[1])
    lane = lax.broadcasted_iota(jnp.int32, (height, LANES), 1)
    strip = LANES // 4
    to_east = jnp.zeros((height, LANES), jnp.float32)
    to_west = jnp.zeros((height, LANES), jnp.float32)
    for f in range(4):
        here = (lane >= f * strip) & (lane < (f + 1) * strip)
        east = fields[f, own_rows, breadth - LANES:]
        west = fields[f, own_rows, :LANES]
        to_east = jnp.where(here, pltpu.roll(east, ((f + 1) * strip) % LANES, 1), to_east)
        to_west = jnp.where(here, pltpu.roll(west, f * strip, 1), to_west)
    pack_out[0] = to_east
    pack_out[1] = to_west
    start_all(field_copy, NEAR)
    loads[5].wait()

    frame_row = lax.broadcasted_iota(jnp.int32, (high, wide), 0)
    frame_lane = lax.broadcasted_iota(jnp.int32, (high, wide), 1)
    grid_row = frame_row - ROWS + x * height
    grid_lane = frame_lane - SIDE + y * breadth
    inside = (
        (grid_row >= 0) & (grid_row < height * gx) & (grid_lane >= 0) & (grid_lane < breadth * gy)
    )
    own_lane = lax.broadcasted_iota(jnp.int32, (height, wide), 1)
    own = (own_lane >= SIDE) & (own_lane < SIDE + breadth)
    line_lane = lax.broadcasted_iota(jnp.int32, (lines, wide), 1)
    in_patch = (line_lane >= SIDE - OV) & (line_lane < SIDE + breadth + OV)
    vector_index = lax.broadcasted_iota(jnp.int32, (vectors, 1), 0)
    live = (vector_index < counts[0, 0]).astype(jnp.float32)
    quarter = lax.rem(seat, 4)
    row_lane = lax.broadcasted_iota(jnp.int32, (1, LANES), 1)
    spot = (
        lax.broadcasted_iota(jnp.int32, (vectors, LANES), 1)
        == lax.broadcasted_iota(jnp.int32, (vectors, LANES), 0) + strip * quarter
    )
    device_row = lax.broadcasted_iota(jnp.int32, (devices, LANES), 0)
    device_lane = lax.broadcasted_iota(jnp.int32, (devices, LANES), 1)
    is_coarse = device_lane // strip == lax.rem(device_row, 4)

    def restrict():
        pieces = None
        for q in range(group):
            taken = jnp.concatenate(
                [
                    total[t, pl.ds(ROWS - OV + q, lines, stride=group), :]
                    for t in range(wide // LANES)
                ],
                axis=1,
            )
            taken = jnp.where(in_patch, taken, 0.0)
            taken = jnp.concatenate(
                [taken, jnp.zeros((lines, length - wide), jnp.float32)], axis=1
            )
            taken = pltpu.roll(taken, (py * q - (SIDE - OV)) % length, 1)
            pieces = taken if pieces is None else pieces + taken
        flat[...] = pieces
        summed = jnp.zeros((vectors, length), jnp.float32)
        for a in range(lines):
            summed = summed + basis[:, a * length:(a + 1) * length] * flat[a:a + 1, :]
        folded = summed[:, :LANES]
        for t in range(1, length // LANES):
            folded = folded + summed[:, t * LANES:(t + 1) * LANES]
        coarse = jnp.sum(folded, axis=1, keepdims=True) * live
        return jnp.sum(jnp.where(spot, coarse, 0.0), axis=0, keepdims=True)

    def spread(rows):
        rows = jnp.where(is_coarse, rows, 0.0)
        joined = rows
        for i in range(1, 4):
            joined = joined + pltpu.roll(rows, i, 0)
        summed = jnp.zeros((vectors, LANES), jnp.float32)
        for b in range(devices // 4):
            first = 4 * b
            device = (first % members) // inner * gy + first // members * inner + first % inner
            summed = (
                summed
                + inverse[:, device * strip:device * strip + LANES] * joined[first + 3:first + 4, :]
            )
        weights = jnp.sum(summed, axis=1, keepdims=True) * live
        weights = jnp.broadcast_to(weights, (vectors, LANES))
        weights = jnp.concatenate([weights] * (length // LANES), axis=1)
        for a in range(lines):
            flat[a:a + 1, :] = jnp.sum(
                basis[:, a * length:(a + 1) * length] * weights, axis=0, keepdims=True
            )
        whole = flat[...]
        for t in range(wide // LANES):
            total[t] = jnp.zeros((high, LANES), jnp.float32)
        for q in range(group):
            moved = pltpu.roll(whole, (SIDE - OV - py * q) % length, 1)[:, :wide]
            moved = jnp.where(in_patch, moved, 0.0)
            for t in range(wide // LANES):
                total[t, pl.ds(ROWS - OV + q, lines, stride=group), :] = (
                    moved[:, t * LANES:(t + 1) * LANES]
                )
        return get_total()

    def set_total(value):
        for t in range(wide // LANES):
            total[t] = value[:, t * LANES:(t + 1) * LANES]

    def get_total():
        return jnp.concatenate([total[t] for t in range(wide // LANES)], axis=1)

    def around(value):
        rows = value.shape[0]
        return (
            pltpu.roll(value, rows - 1, 0),
            pltpu.roll(value, 1, 0),
            pltpu.roll(value, wide - 1, 1),
            pltpu.roll(value, 1, 1),
        )

    def exchange(turn):
        start_all(part_copy(turn), directions[turn])
        set_total(part[turn])
        receive_all(part_copy(turn), directions[turn])
        for number, (di, dj) in enumerate(directions[turn]):
            _, _, rows, columns = part_slices(turn, di, dj, height, breadth)
            got = arrived[turn][number][...]
            first = columns.start // LANES
            for t in range(columns.size // LANES):
                total[first + t, rows, :] = (
                    total[first + t, rows, :] + got[:, t * LANES:(t + 1) * LANES]
                )
        return jnp.where(inside, get_total(), 0.0)

    def dots(pairs):
        row = jnp.zeros((1, LANES), jnp.float32)
        place = lax.rem(quarter + 1, 4) * strip
        for i, (one, other) in enumerate(pairs):
            product = jnp.sum(jnp.where(own, one * other, 0.0), axis=0, keepdims=True)
            value = jnp.sum(product, axis=1, keepdims=True)
            row = jnp.where(row_lane == place + i, value, row)
        return row

    def whole_sums(rows, count):
        others = jnp.where(is_coarse, 0.0, rows)
        row = jnp.sum(others, axis=0, keepdims=True)
        return [
            jnp.sum(jnp.where(lax.rem(row_lane, strip) == i, row, 0.0), axis=1, keepdims=True)
            for i in range(count)
        ]

    receive_all(source_copy, NEAR)
    first_vector = pltpu.roll(grown[...], wide + LANES - SIDE, 1)[:, :wide]
    set_total(first_vector)
    loads[7].wait()
    row_out[0] = restrict()
    share(0)

    receive_all(field_copy, NEAR)
    patch = []
    side_lane = lax.broadcasted_iota(jnp.int32, (high, LANES), 1)
    for f in range(4):
        base = jnp.concatenate([fields[f], jnp.zeros((high, LANES), jnp.float32)], axis=1)
        base = pltpu.roll(base, SIDE, 1)
        west = pltpu.roll(pack_in[0], (SIDE - (f + 1) * strip) % LANES, 1)
        east = pltpu.roll(pack_in[1], (SIDE - f * strip) % LANES, 1)
        left = jnp.where((side_lane >= SIDE - strip) & (side_lane < SIDE), west, base[:, :LANES])
        right = jnp.where(
            (side_lane >= SIDE) & (side_lane < SIDE + strip), east, base[:, wide - LANES:]
        )
        patch.append(jnp.concatenate([left, base[:, LANES:wide - LANES], right], axis=1))
    level = jnp.exp(0.5 * patch[0])
    level_inverse = jnp.exp(-0.5 * patch[0])
    root_along, root_across = patch[1], patch[2]
    faces = (
        root_along * pltpu.roll(root_along, high - 1, 0),
        root_along * pltpu.roll(root_along, 1, 0),
        root_across * pltpu.roll(root_across, wide - 1, 1),
        root_across * pltpu.roll(root_across, 1, 1),
    )
    outflow = jnp.zeros((high, wide), jnp.float32)
    for face, beside in zip(faces, around(level_inverse)):
        outflow = outflow + face * beside
    diagonal = patch[3] + level * outflow
    diagonal = jnp.where(diagonal > 0.0, diagonal, 1.0)
    near = slice(ROWS - NARROW, ROWS + height + NARROW)
    middle = slice(NARROW, NARROW + height)
    mine = slice(ROWS, ROWS + height)
    step_size = OMEGA / diagonal[near]
    step_faces = [face[near] * step_size for face in faces]
    step_level = step_size * level[near]
    own_level_inverse = level_inverse[mine]

    def smooth(vector, turn):
        scaled = step_level * vector[near]
        field = scaled
        for sweep in range(SWEEPS - 1):
            if sweep == 2 * turn:
                pass_on(turn)
            moved = (1.0 - OMEGA) * field + scaled
            for face, beside in zip(step_faces, around(field)):
                moved = moved + face * beside
            field = moved
        return jnp.where(own, own_level_inverse * field[middle], 0.0)

    def apply(vector, rows):
        scaled = level[rows] * vector
        image = diagonal[rows] * scaled
        for face, beside in zip(faces, around(scaled)):
            image = image - face[rows] * beside
        return level_inverse[rows] * image

    def put_part(turn, solved, spreads):
        part[turn] = spreads
        part[turn, own_rows, :] = spreads[mine] + solved

    solved = smooth(first_vector, 0)
    loads[6].wait()
    put_part(0, solved, spread(collect(0)))
    first_dir = exchange(0)
    image = apply(first_dir, slice(0, high))

    set_total(image)
    first_vector_own, image_own = first_vector[mine], image[mine]
    row_out[1] = restrict() + dots(
        [
            (first_vector_own, first_vector_own),
            (first_vector_own, image_own),
            (image_own, image_own),
        ]
    )
    share(1)
    solved = smooth(image, 1)
    rows = collect(1)
    put_part(1, solved, spread(rows))
    second_dir = exchange(1)[near]
    first_dir, first_vector, image = first_dir[near], first_vector[near], image[near]
    squares, mixed, image_squares = whole_sums(rows, 3)
    source_norm = jnp.sqrt(squares + EPSILON)
    shrink = 1.0 / source_norm
    first_first = mixed * shrink * shrink
    left_over = (
        image_squares * shrink * shrink
        - 2.0 * first_first * first_first
        + first_first * first_first * (squares * shrink * shrink)
    )
    second_first = jnp.sqrt(jnp.maximum(left_over, 0.0) + EPSILON)
    first = first_vector * shrink
    first_dir = first_dir * shrink
    second = (image * shrink - first_first * first) / second_first
    second_dir = (second_dir * shrink - first_first * first_dir) / second_first
    image = apply(second_dir, near)[middle]
    first_dir, second_dir = first_dir[middle], second_dir[middle]
    first, second = first[middle], second[middle]
    row_out[2] = dots(
        [(first, image), (second, image), (image, image), (first, first), (second, second),
         (first, second)]
    )
    share(2)
    pass_on(2)
    first_second, second_second, image_squares, ones, twos, cross = whole_sums(collect(2), 6)
    left_over = (
        image_squares
        - 2.0 * (first_second * first_second + second_second * second_second)
        + first_second * first_second * ones
        + second_second * second_second * twos
        + 2.0 * first_second * second_second * cross
    )
    third_second = jnp.sqrt(jnp.maximum(left_over, 0.0) + EPSILON)
    image = image - first_second * first - second_second * second
    weight_one, weight_two, remainder_one, remainder_two, remainder_three = least_squares(
        source_norm, first_first, second_first, first_second, second_second, third_second
    )
    answer = weight_one * first_dir + weight_two * second_dir
    remainder = (
        remainder_one * first + remainder_two * second + (remainder_three / third_second) * image
    )
    solution_out[...] = pltpu.roll(answer, wide - SIDE, 1)[:, :breadth]
    residual_out[...] = pltpu.roll(remainder, wide - SIDE, 1)[:, :breadth]

    sent_all(source_copy, NEAR)
    sent_all(field_copy, NEAR)
    for turn in range(2):
        sent_all(part_copy(turn), directions[turn])
    for turn in range(3):
        row_bytes(turn, members - 1, row_send).wait()
        row_bytes(turn, devices - members, block_send).wait()


def on_device(
    gx, gy,
    source, potential, mobility_along, mobility_across, recombination, counts, basis, coarse_inverse
):
    height, breadth = source.shape
    vectors = basis.shape[0]
    devices = gx * gy
    high, wide = height + 2 * ROWS, breadth + 2 * SIDE
    px, py = height + 2 * OV, breadth + 2 * OV
    group = LANES // math.gcd(py, LANES)
    far = FAR if gx > 2 else []
    arrived = []
    for turn, chosen in enumerate((NEAR + far, NEAR)):
        for di, dj in chosen:
            rows, columns, _, _ = part_slices(turn, di, dj, height, breadth)
            arrived.append(pltpu.VMEM((rows.size, columns.size), jnp.float32))
    vmem = pl.BlockSpec(memory_space=pltpu.VMEM)
    hbm = pl.BlockSpec(memory_space=pltpu.HBM)
    ways = len(NEAR + far)
    return pl.pallas_call(
        functools.partial(kernel, gx, gy, far),
        out_shape=(
            jax.ShapeDtypeStruct((height, breadth), jnp.float32),
            jax.ShapeDtypeStruct((height, breadth), jnp.float32),
        ),
        in_specs=[hbm] * 8,
        out_specs=(vmem, vmem),
        scratch_shapes=[
            pltpu.SMEM((1, 1), jnp.int32),
            pltpu.VMEM(basis.shape, jnp.float32),
            pltpu.VMEM(coarse_inverse.shape, jnp.float32),
            pltpu.VMEM((high, breadth + 2 * LANES), jnp.float32),
            pltpu.VMEM((2, height, breadth), jnp.float32),
            pltpu.VMEM((4, high, breadth), jnp.float32),
            pltpu.VMEM((2, height, LANES), jnp.float32),
            pltpu.VMEM((2, high, LANES), jnp.float32),
            pltpu.VMEM((2, high, wide), jnp.float32),
            pltpu.VMEM((wide // LANES, high, LANES), jnp.float32),
            pltpu.VMEM((px // group, py * group), jnp.float32),
            pltpu.VMEM((3, 1, LANES), jnp.float32),
            pltpu.VMEM((3, devices, 1, LANES), jnp.float32),
            *arrived,
            pltpu.SemaphoreType.DMA((8,)),
            pltpu.SemaphoreType.DMA((4, ways)),
            pltpu.SemaphoreType.DMA((4, ways)),
            pltpu.SemaphoreType.DMA((3,)),
            pltpu.SemaphoreType.DMA((3,)),
            pltpu.SemaphoreType.DMA((3,)),
            pltpu.SemaphoreType.DMA((3,)),
        ],
        compiler_params=pltpu.CompilerParams(
            collective_id=0, has_side_effects=True, vmem_limit_bytes=VMEM_GRANT
        ),
    )(counts, source, potential, mobility_along, mobility_across, recombination, basis, coarse_inverse)


def solution(mesh):
    placed = (P("gx", "gy"),) * 7 + (P(("gx", "gy"), None),)
    return jax.shard_map(
        functools.partial(on_device, mesh.shape["gx"], mesh.shape["gy"]),
        mesh=mesh,
        in_specs=placed,
        out_specs=(P("gx", "gy"), P("gx", "gy")),
        check_vma=False,
    )
```

```python
import functools
import math
import jax
import jax.numpy as jnp
from jax import lax
from jax.experimental import pallas as pl
from jax.experimental.pallas import tpu as pltpu
from jax.sharding import PartitionSpec as P

OV = 16
SWEEPS = 8
OMEGA = 0.8
EPSILON = 1e-06
LANES = 128
ROWS = 24
SIDE = 64
NARROW = 8
VMEM_GRANT = 63 * 1024 * 1024
MESH = pl.DeviceIdType.MESH

NEAR = [(i, j) for i in (-1, 0, 1) for j in (-1, 0, 1) if (i, j) != (0, 0)]
FAR = [(i, j) for i in (-2, 2) for j in (-1, 0, 1)]


def least_squares(
    source_norm, first_first, second_first, first_second, second_second, third_second
):
    radius = jnp.sqrt(first_first * first_first + second_first * second_first)
    cosine = first_first / radius
    sine = second_first / radius
    upper_right = cosine * first_second + sine * second_second
    lower_right = cosine * second_second - sine * first_second
    radius_two = jnp.sqrt(lower_right * lower_right + third_second * third_second)
    weight_two = lower_right / radius_two * (-sine * source_norm) / radius_two
    weight_one = (cosine * source_norm - upper_right * weight_two) / radius
    remainder_one = source_norm - first_first * weight_one - first_second * weight_two
    remainder_two = -second_first * weight_one - second_second * weight_two
    remainder_three = -third_second * weight_two
    return (weight_one, weight_two, remainder_one, remainder_two, remainder_three)


def part_slices(turn, di, dj, height, breadth):
    high, wide = height + 2 * ROWS, breadth + 2 * SIDE
    margin = ROWS - OV
    reach = ROWS if turn == 0 else NARROW
    if di == 0:
        used = min(reach, OV)
        start, size, to = ROWS - used, height + 2 * used, ROWS - used
    elif di == 1:
        start, size, to = height + ROWS - reach, reach + OV, ROWS - reach
    elif di == -1:
        start, size, to = margin, reach + OV, ROWS + height - OV
    elif di == 2:
        start, size, to = 2 * height, margin, 0
    else:
        start, size, to = margin, margin, high - margin
    if dj == 0:
        lane, width, lane_to = 0, wide, 0
    elif dj == 1:
        lane, width, lane_to = wide - LANES, LANES, 0
    else:
        lane, width, lane_to = 0, LANES, wide - LANES
    return (pl.ds(start, size), pl.ds(lane, width), pl.ds(to, size), pl.ds(lane_to, width))


def kernel(
    gx, gy, far,
    counts_hbm, source, potential, along, across, recombination, basis_hbm, inverse_hbm,
    both_out,
    counts, basis, inverse, grown, raw, fields, pack_out, pack_in, part, total, flat, row_out,
    gathered, *rest,
):
    directions = (NEAR + far, NEAR)
    arrived = (rest[: len(directions[0])], rest[len(directions[0]):][: len(NEAR)])
    load_sem, send_sem, recv_sem, row_send, row_recv = rest[len(directions[0]) + len(NEAR):]
    devices = gx * gy
    x = lax.axis_index("gx")
    y = lax.axis_index("gy")
    me = x * gy + y
    height, breadth = source.shape
    vectors = basis.shape[0]
    high, wide = height + 2 * ROWS, breadth + 2 * SIDE
    px, py = height + 2 * OV, breadth + 2 * OV
    group = LANES // math.gcd(py, LANES)
    lines, length = px // group, py * group
    own_rows = pl.ds(ROWS, height)

    def wrapped(place, step, size):
        return jnp.where(place + step >= size, place + step - size, place + step)

    few = devices <= 64
    along_x = [wrapped(x, a, gx) if a else x for a in range(gx)]
    along_y = [wrapped(y, b, gy) if b else y for b in range(gy)] if few else []

    def to_others(act):
        for a in range(gx):
            if few:
                for b in range(gy):
                    if a or b:
                        act((along_x[a], along_y[b]))
            else:
                def step(b, carry, a=a):
                    act((along_x[a], wrapped(y, b, gy)))
                    return carry

                lax.fori_loop(0 if a else 1, gy, step, 0)

    sources = [
        (source, grown.at[own_rows, pl.ds(LANES, breadth)]),
        (potential, fields.at[0, own_rows, :]),
        (along, raw.at[0]),
        (across, raw.at[1]),
        (recombination, fields.at[3, own_rows, :]),
        (counts_hbm, counts),
        (inverse_hbm, inverse),
        (basis_hbm, basis),
    ]
    loads = [
        pltpu.make_async_copy(src, dst, load_sem.at[i]) for i, (src, dst) in enumerate(sources)
    ]
    for load in loads:
        load.start()
    barrier = pltpu.get_barrier_semaphore()
    to_others(
        lambda place: pl.semaphore_signal(barrier, inc=1, device_id=place, device_id_type=MESH)
    )

    def present(di, dj):
        return (x + di >= 0) & (x + di < gx) & (y + dj >= 0) & (y + dj < gy)

    def copy(src, dst, phase, number, di, dj):
        return pltpu.make_async_remote_copy(
            src_ref=src,
            dst_ref=dst,
            send_sem=send_sem.at[phase, number],
            recv_sem=recv_sem.at[phase, number],
            device_id=(x + di, y + dj),
            device_id_type=MESH,
        )

    def source_target(di, dj):
        start, size, to = {
            0: (0, height, ROWS),
            1: (height - OV, OV, ROWS - OV),
            -1: (0, OV, ROWS + height),
        }[di]
        column, width, column_to = {
            0: (0, breadth, LANES),
            1: (breadth - LANES, LANES, 0),
            -1: (0, LANES, LANES + breadth),
        }[dj]
        return (
            grown.at[pl.ds(ROWS + start, size), pl.ds(LANES + column, width)],
            grown.at[pl.ds(to, size), pl.ds(column_to, width)],
        )

    def field_target(di, dj):
        start, size, to = {
            0: (0, height, ROWS),
            1: (height - ROWS, ROWS, 0),
            -1: (0, ROWS, ROWS + height),
        }[di]
        if dj == 0:
            return (
                fields.at[:, pl.ds(ROWS + start, size), :], fields.at[:, pl.ds(to, size), :]
            )
        side = 0 if dj == 1 else 1
        return (pack_out.at[side, pl.ds(start, size), :], pack_in.at[side, pl.ds(to, size), :])

    def source_copy(number, di, dj):
        return copy(*source_target(di, dj), 0, number, di, dj)

    def field_copy(number, di, dj):
        return copy(*field_target(di, dj), 1, number, di, dj)

    def part_copy(turn):
        def make(number, di, dj):
            rows, columns, _, _ = part_slices(turn, di, dj, height, breadth)
            return copy(
                part.at[turn, rows, columns], arrived[turn][number], 2 + turn, number, di, dj
            )

        return make

    def start_all(make, chosen):
        for number, (di, dj) in enumerate(chosen):
            @pl.when(present(di, dj))
            def _(number=number, di=di, dj=dj):
                make(number, di, dj).start()

    def receive_all(make, chosen):
        for number, (di, dj) in enumerate(chosen):
            @pl.when(present(-di, -dj))
            def _(number=number, di=di, dj=dj):
                make(number, di, dj).wait_recv()

    def sent_all(make, chosen):
        for number, (di, dj) in enumerate(chosen):
            @pl.when(present(di, dj))
            def _(number=number, di=di, dj=dj):
                make(number, di, dj).wait_send()

    def share(turn):
        gathered[turn, me] = row_out[turn]
        to_others(
            lambda place: pltpu.make_async_remote_copy(
                src_ref=row_out.at[turn],
                dst_ref=gathered.at[turn, me],
                send_sem=row_send.at[turn],
                recv_sem=row_recv.at[turn],
                device_id=place,
                device_id_type=MESH,
            ).start()
        )

    def row_bytes(turn, sem):
        some = gathered.at[turn, pl.ds(0, devices - 1)]
        return pltpu.make_async_copy(some, some, sem.at[turn])

    def collect(turn):
        row_bytes(turn, row_recv).wait()
        return gathered[turn].reshape(devices, LANES)

    for number, (di, dj) in enumerate(directions[0]):
        @pl.when(jnp.logical_not(present(-di, -dj)))
        def _(number=number, di=di, dj=dj):
            targets = [arrived[0][number]]
            if (di, dj) in NEAR:
                targets += [
                    arrived[1][number], source_target(di, dj)[1], field_target(di, dj)[1]
                ]
            for target in targets:
                target[...] = jnp.zeros(target.shape, jnp.float32)

    unused = jnp.zeros((ROWS - OV, breadth + 2 * LANES), jnp.float32)
    grown[: ROWS - OV, :] = unused
    grown[high - ROWS + OV:, :] = unused

    loads[0].wait()
    pl.semaphore_wait(barrier, devices - 1)
    start_all(source_copy, NEAR)

    for load in loads[1:5]:
        load.wait()
    fields[1, own_rows, :] = jnp.sqrt(raw[0])
    fields[2, own_rows, :] = jnp.sqrt(raw[1])
    lane = lax.broadcasted_iota(jnp.int32, (height, LANES), 1)
    strip = LANES // 4
    to_east = jnp.zeros((height, LANES), jnp.float32)
    to_west = jnp.zeros((height, LANES), jnp.float32)
    for f in range(4):
        here = (lane >= f * strip) & (lane < (f + 1) * strip)
        east = fields[f, own_rows, breadth - LANES:]
        west = fields[f, own_rows, :LANES]
        to_east = jnp.where(here, pltpu.roll(east, ((f + 1) * strip) % LANES, 1), to_east)
        to_west = jnp.where(here, pltpu.roll(west, f * strip, 1), to_west)
    pack_out[0] = to_east
    pack_out[1] = to_west
    start_all(field_copy, NEAR)
    loads[5].wait()

    frame_row = lax.broadcasted_iota(jnp.int32, (high, wide), 0)
    frame_lane = lax.broadcasted_iota(jnp.int32, (high, wide), 1)
    grid_row = frame_row - ROWS + x * height
    grid_lane = frame_lane - SIDE + y * breadth
    inside = (
        (grid_row >= 0) & (grid_row < height * gx) & (grid_lane >= 0) & (grid_lane < breadth * gy)
    )
    own_lane = lax.broadcasted_iota(jnp.int32, (height, wide), 1)
    own = (own_lane >= SIDE) & (own_lane < SIDE + breadth)
    line_lane = lax.broadcasted_iota(jnp.int32, (lines, wide), 1)
    in_patch = (line_lane >= SIDE - OV) & (line_lane < SIDE + breadth + OV)
    vector_index = lax.broadcasted_iota(jnp.int32, (vectors, 1), 0)
    live = (vector_index < counts[0, 0]).astype(jnp.float32)
    quarter = lax.rem(me, 4)
    row_lane = lax.broadcasted_iota(jnp.int32, (1, LANES), 1)
    spot = (
        lax.broadcasted_iota(jnp.int32, (vectors, LANES), 1)
        == lax.broadcasted_iota(jnp.int32, (vectors, LANES), 0) + strip * quarter
    )
    device_row = lax.broadcasted_iota(jnp.int32, (devices, LANES), 0)
    device_lane = lax.broadcasted_iota(jnp.int32, (devices, LANES), 1)
    is_coarse = device_lane // strip == lax.rem(device_row, 4)

    def restrict():
        pieces = None
        for q in range(group):
            taken = jnp.concatenate(
                [
                    total[t, pl.ds(ROWS - OV + q, lines, stride=group), :]
                    for t in range(wide // LANES)
                ],
                axis=1,
            )
            taken = jnp.where(in_patch, taken, 0.0)
            taken = jnp.concatenate(
                [taken, jnp.zeros((lines, length - wide), jnp.float32)], axis=1
            )
            taken = pltpu.roll(taken, (py * q - (SIDE - OV)) % length, 1)
            pieces = taken if pieces is None else pieces + taken
        flat[...] = pieces
        summed = jnp.zeros((vectors, length), jnp.float32)
        for a in range(lines):
            summed = summed + basis[:, a * length:(a + 1) * length] * flat[a:a + 1, :]
        folded = summed[:, :LANES]
        for t in range(1, length // LANES):
            folded = folded + summed[:, t * LANES:(t + 1) * LANES]
        coarse = jnp.sum(folded, axis=1, keepdims=True) * live
        return jnp.sum(jnp.where(spot, coarse, 0.0), axis=0, keepdims=True)

    def spread(rows):
        rows = jnp.where(is_coarse, rows, 0.0)
        joined = rows
        for i in range(1, 4):
            joined = joined + pltpu.roll(rows, i, 0)
        summed = jnp.zeros((vectors, LANES), jnp.float32)
        for b in range(devices // 4):
            summed = (
                summed + inverse[:, b * LANES:(b + 1) * LANES] * joined[4 * b + 3:4 * b + 4, :]
            )
        weights = jnp.sum(summed, axis=1, keepdims=True) * live
        weights = jnp.broadcast_to(weights, (vectors, LANES))
        weights = jnp.concatenate([weights] * (length // LANES), axis=1)
        for a in range(lines):
            flat[a:a + 1, :] = jnp.sum(
                basis[:, a * length:(a + 1) * length] * weights, axis=0, keepdims=True
            )
        whole = flat[...]
        for t in range(wide // LANES):
            total[t] = jnp.zeros((high, LANES), jnp.float32)
        for q in range(group):
            moved = pltpu.roll(whole, (SIDE - OV - py * q) % length, 1)[:, :wide]
            moved = jnp.where(in_patch, moved, 0.0)
            for t in range(wide // LANES):
                total[t, pl.ds(ROWS - OV + q, lines, stride=group), :] = (
                    moved[:, t * LANES:(t + 1) * LANES]
                )
        return get_total()

    def set_total(value):
        for t in range(wide // LANES):
            total[t] = value[:, t * LANES:(t + 1) * LANES]

    def get_total():
        return jnp.concatenate([total[t] for t in range(wide // LANES)], axis=1)

    def around(value):
        rows = value.shape[0]
        return (
            pltpu.roll(value, rows - 1, 0),
            pltpu.roll(value, 1, 0),
            pltpu.roll(value, wide - 1, 1),
            pltpu.roll(value, 1, 1),
        )

    def exchange(turn):
        start_all(part_copy(turn), directions[turn])
        set_total(part[turn])
        receive_all(part_copy(turn), directions[turn])
        for number, (di, dj) in enumerate(directions[turn]):
            _, _, rows, columns = part_slices(turn, di, dj, height, breadth)
            got = arrived[turn][number][...]
            first = columns.start // LANES
            for t in range(columns.size // LANES):
                total[first + t, rows, :] = (
                    total[first + t, rows, :] + got[:, t * LANES:(t + 1) * LANES]
                )
        return jnp.where(inside, get_total(), 0.0)

    def dots(pairs):
        row = jnp.zeros((1, LANES), jnp.float32)
        place = lax.rem(quarter + 1, 4) * strip
        for i, (one, other) in enumerate(pairs):
            product = jnp.sum(jnp.where(own, one * other, 0.0), axis=0, keepdims=True)
            value = jnp.sum(product, axis=1, keepdims=True)
            row = jnp.where(row_lane == place + i, value, row)
        return row

    def whole_sums(rows, count):
        others = jnp.where(is_coarse, 0.0, rows)
        row = jnp.sum(others, axis=0, keepdims=True)
        return [
            jnp.sum(jnp.where(lax.rem(row_lane, strip) == i, row, 0.0), axis=1, keepdims=True)
            for i in range(count)
        ]

    receive_all(source_copy, NEAR)
    first_vector = pltpu.roll(grown[...], wide + LANES - SIDE, 1)[:, :wide]
    set_total(first_vector)
    loads[7].wait()
    row_out[0] = restrict()
    share(0)

    receive_all(field_copy, NEAR)
    patch = []
    side_lane = lax.broadcasted_iota(jnp.int32, (high, LANES), 1)
    for f in range(4):
        base = jnp.concatenate([fields[f], jnp.zeros((high, LANES), jnp.float32)], axis=1)
        base = pltpu.roll(base, SIDE, 1)
        west = pltpu.roll(pack_in[0], (SIDE - (f + 1) * strip) % LANES, 1)
        east = pltpu.roll(pack_in[1], (SIDE - f * strip) % LANES, 1)
        left = jnp.where((side_lane >= SIDE - strip) & (side_lane < SIDE), west, base[:, :LANES])
        right = jnp.where(
            (side_lane >= SIDE) & (side_lane < SIDE + strip), east, base[:, wide - LANES:]
        )
        patch.append(jnp.concatenate([left, base[:, LANES:wide - LANES], right], axis=1))
    level = jnp.exp(0.5 * patch[0])
    level_inverse = jnp.exp(-0.5 * patch[0])
    root_along, root_across = patch[1], patch[2]
    faces = (
        root_along * pltpu.roll(root_along, high - 1, 0),
        root_along * pltpu.roll(root_along, 1, 0),
        root_across * pltpu.roll(root_across, wide - 1, 1),
        root_across * pltpu.roll(root_across, 1, 1),
    )
    outflow = jnp.zeros((high, wide), jnp.float32)
    for face, beside in zip(faces, around(level_inverse)):
        outflow = outflow + face * beside
    diagonal = patch[3] + level * outflow
    diagonal = jnp.where(diagonal > 0.0, diagonal, 1.0)
    near = slice(ROWS - NARROW, ROWS + height + NARROW)
    middle = slice(NARROW, NARROW + height)
    mine = slice(ROWS, ROWS + height)
    step_size = OMEGA / diagonal[near]
    step_faces = [face[near] * step_size for face in faces]
    step_level = step_size * level[near]
    own_level_inverse = level_inverse[mine]

    def smooth(vector):
        scaled = step_level * vector[near]
        field = scaled
        for sweep in range(SWEEPS - 1):
            moved = (1.0 - OMEGA) * field + scaled
            for face, beside in zip(step_faces, around(field)):
                moved = moved + face * beside
            field = moved
        return jnp.where(own, own_level_inverse * field[middle], 0.0)

    def apply(vector, rows):
        scaled = level[rows] * vector
        image = diagonal[rows] * scaled
        for face, beside in zip(faces, around(scaled)):
            image = image - face[rows] * beside
        return level_inverse[rows] * image

    def put_part(turn, solved, spreads):
        part[turn] = spreads
        part[turn, own_rows, :] = spreads[mine] + solved

    solved = smooth(first_vector)
    loads[6].wait()
    put_part(0, solved, spread(collect(0)))
    first_dir = exchange(0)
    image = apply(first_dir, slice(0, high))

    set_total(image)
    first_vector_own, image_own = first_vector[mine], image[mine]
    row_out[1] = restrict() + dots(
        [
            (first_vector_own, first_vector_own),
            (first_vector_own, image_own),
            (image_own, image_own),
        ]
    )
    share(1)
    solved = smooth(image)
    rows = collect(1)
    put_part(1, solved, spread(rows))
    second_dir = exchange(1)[near]
    first_dir, first_vector, image = first_dir[near], first_vector[near], image[near]
    squares, mixed, image_squares = whole_sums(rows, 3)
    source_norm = jnp.sqrt(squares + EPSILON)
    shrink = 1.0 / source_norm
    first_first = mixed * shrink * shrink
    left_over = (
        image_squares * shrink * shrink
        - 2.0 * first_first * first_first
        + first_first * first_first * (squares * shrink * shrink)
    )
    second_first = jnp.sqrt(jnp.maximum(left_over, 0.0) + EPSILON)
    first = first_vector * shrink
    first_dir = first_dir * shrink
    second = (image * shrink - first_first * first) / second_first
    second_dir = (second_dir * shrink - first_first * first_dir) / second_first
    image = apply(second_dir, near)[middle]
    first_dir, second_dir = first_dir[middle], second_dir[middle]
    first, second = first[middle], second[middle]
    row_out[2] = dots(
        [(first, image), (second, image), (image, image), (first, first), (second, second),
         (first, second)]
    )
    share(2)
    first_second, second_second, image_squares, ones, twos, cross = whole_sums(collect(2), 6)
    left_over = (
        image_squares
        - 2.0 * (first_second * first_second + second_second * second_second)
        + first_second * first_second * ones
        + second_second * second_second * twos
        + 2.0 * first_second * second_second * cross
    )
    third_second = jnp.sqrt(jnp.maximum(left_over, 0.0) + EPSILON)
    image = image - first_second * first - second_second * second
    weight_one, weight_two, remainder_one, remainder_two, remainder_three = least_squares(
        source_norm, first_first, second_first, first_second, second_second, third_second
    )
    answer = weight_one * first_dir + weight_two * second_dir
    remainder = (
        remainder_one * first + remainder_two * second + (remainder_three / third_second) * image
    )
    both_out[0] = pltpu.roll(answer, wide - SIDE, 1)[:, :breadth]
    both_out[1] = pltpu.roll(remainder, wide - SIDE, 1)[:, :breadth]

    sent_all(source_copy, NEAR)
    sent_all(field_copy, NEAR)
    for turn in range(2):
        sent_all(part_copy(turn), directions[turn])
    for turn in range(3):
        row_bytes(turn, row_send).wait()


def on_device(
    gx, gy,
    source, potential, mobility_along, mobility_across, recombination, counts, basis, coarse_inverse
):
    height, breadth = source.shape
    vectors = basis.shape[0]
    devices = gx * gy
    high, wide = height + 2 * ROWS, breadth + 2 * SIDE
    px, py = height + 2 * OV, breadth + 2 * OV
    group = LANES // math.gcd(py, LANES)
    far = FAR if gx > 2 else []
    arrived = []
    for turn, chosen in enumerate((NEAR + far, NEAR)):
        for di, dj in chosen:
            rows, columns, _, _ = part_slices(turn, di, dj, height, breadth)
            arrived.append(pltpu.VMEM((rows.size, columns.size), jnp.float32))
    vmem = pl.BlockSpec(memory_space=pltpu.VMEM)
    hbm = pl.BlockSpec(memory_space=pltpu.HBM)
    ways = len(NEAR + far)
    both = pl.pallas_call(
        functools.partial(kernel, gx, gy, far),
        out_shape=jax.ShapeDtypeStruct((2, height, breadth), jnp.float32),
        in_specs=[hbm] * 8,
        out_specs=vmem,
        scratch_shapes=[
            pltpu.SMEM((1, 1), jnp.int32),
            pltpu.VMEM(basis.shape, jnp.float32),
            pltpu.VMEM(coarse_inverse.shape, jnp.float32),
            pltpu.VMEM((high, breadth + 2 * LANES), jnp.float32),
            pltpu.VMEM((2, height, breadth), jnp.float32),
            pltpu.VMEM((4, high, breadth), jnp.float32),
            pltpu.VMEM((2, height, LANES), jnp.float32),
            pltpu.VMEM((2, high, LANES), jnp.float32),
            pltpu.VMEM((2, high, wide), jnp.float32),
            pltpu.VMEM((wide // LANES, high, LANES), jnp.float32),
            pltpu.VMEM((px // group, py * group), jnp.float32),
            pltpu.VMEM((3, 1, LANES), jnp.float32),
            pltpu.VMEM((3, devices, 1, LANES), jnp.float32),
            *arrived,
            pltpu.SemaphoreType.DMA((8,)),
            pltpu.SemaphoreType.DMA((4, ways)),
            pltpu.SemaphoreType.DMA((4, ways)),
            pltpu.SemaphoreType.DMA((3,)),
            pltpu.SemaphoreType.DMA((3,)),
        ],
        compiler_params=pltpu.CompilerParams(
            collective_id=0, has_side_effects=True, vmem_limit_bytes=VMEM_GRANT
        ),
    )(counts, source, potential, mobility_along, mobility_across, recombination, basis, coarse_inverse)
    return both[0], both[1]


def solution(mesh):
    placed = (P("gx", "gy"),) * 7 + (P(("gx", "gy"), None),)
    return jax.shard_map(
        functools.partial(on_device, mesh.shape["gx"], mesh.shape["gy"]),
        mesh=mesh,
        in_specs=placed,
        out_specs=(P("gx", "gy"), P("gx", "gy")),
        check_vma=False,
    )
```

```python
import functools
import math
import jax
import jax.numpy as jnp
from jax import lax
from jax.experimental import pallas as pl
from jax.experimental.pallas import tpu as pltpu
from jax.sharding import PartitionSpec as P

OV = 16
SWEEPS = 8
OMEGA = 0.8
EPSILON = 1e-06
LANES = 128
ROWS = 24
SIDE = 64
NARROW = 8
VMEM_GRANT = 63 * 1024 * 1024
MESH = pl.DeviceIdType.MESH

NEAR = [(i, j) for i in (-1, 0, 1) for j in (-1, 0, 1) if (i, j) != (0, 0)]
FAR = [(i, j) for i in (-2, 2) for j in (-1, 0, 1)]


def part_slices(turn, di, dj, height, breadth):
    high, wide = height + 2 * ROWS, breadth + 2 * SIDE
    margin = ROWS - OV
    reach = ROWS if turn == 0 else NARROW
    if di == 0:
        used = min(reach, OV)
        start, size, to = ROWS - used, height + 2 * used, ROWS - used
    elif di == 1:
        start, size, to = height + ROWS - reach, reach + OV, ROWS - reach
    elif di == -1:
        start, size, to = margin, reach + OV, ROWS + height - OV
    elif di == 2:
        start, size, to = 2 * height, margin, 0
    else:
        start, size, to = margin, margin, high - margin
    if dj == 0:
        lane, width, lane_to = 0, wide, 0
    elif dj == 1:
        lane, width, lane_to = wide - LANES, LANES, 0
    else:
        lane, width, lane_to = 0, LANES, wide - LANES
    return (pl.ds(start, size), pl.ds(lane, width), pl.ds(to, size), pl.ds(lane_to, width))


def kernel(
    gx, gy, far,
    counts_hbm, source, potential, along, across, recombination, basis_hbm, inverse_hbm,
    both_out,
    counts, basis, inverse, grown, raw, fields, pack_out, pack_in, part, total, flat, row_out,
    gathered, *rest,
):
    directions = (NEAR + far, NEAR)
    arrived = (rest[: len(directions[0])], rest[len(directions[0]):][: len(NEAR)])
    load_sem, send_sem, recv_sem, row_send, row_recv = rest[len(directions[0]) + len(NEAR):]
    devices = gx * gy
    x = lax.axis_index("gx")
    y = lax.axis_index("gy")
    me = x * gy + y
    height, breadth = source.shape
    vectors = basis.shape[0]
    high, wide = height + 2 * ROWS, breadth + 2 * SIDE
    px, py = height + 2 * OV, breadth + 2 * OV
    group = LANES // math.gcd(py, LANES)
    lines, length = px // group, py * group
    own_rows = pl.ds(ROWS, height)

    def wrapped(place, step, size):
        return jnp.where(place + step >= size, place + step - size, place + step)

    few = devices <= 64
    along_x = [wrapped(x, a, gx) if a else x for a in range(gx)]
    along_y = [wrapped(y, b, gy) if b else y for b in range(gy)] if few else []

    def to_others(act):
        for a in range(gx):
            if few:
                for b in range(gy):
                    if a or b:
                        act((along_x[a], along_y[b]))
            else:
                def step(b, carry, a=a):
                    act((along_x[a], wrapped(y, b, gy)))
                    return carry

                lax.fori_loop(0 if a else 1, gy, step, 0)

    sources = [
        (source, grown.at[own_rows, pl.ds(LANES, breadth)]),
        (potential, fields.at[0, own_rows, :]),
        (along, raw.at[0]),
        (across, raw.at[1]),
        (recombination, fields.at[3, own_rows, :]),
        (counts_hbm, counts),
        (inverse_hbm, inverse),
        (basis_hbm, basis),
    ]
    loads = [
        pltpu.make_async_copy(src, dst, load_sem.at[i]) for i, (src, dst) in enumerate(sources)
    ]
    for load in loads:
        load.start()
    barrier = pltpu.get_barrier_semaphore()
    to_others(
        lambda place: pl.semaphore_signal(barrier, inc=1, device_id=place, device_id_type=MESH)
    )

    def present(di, dj):
        return (x + di >= 0) & (x + di < gx) & (y + dj >= 0) & (y + dj < gy)

    def copy(src, dst, phase, number, di, dj):
        return pltpu.make_async_remote_copy(
            src_ref=src,
            dst_ref=dst,
            send_sem=send_sem.at[phase, number],
            recv_sem=recv_sem.at[phase, number],
            device_id=(x + di, y + dj),
            device_id_type=MESH,
        )

    def source_target(di, dj):
        start, size, to = {
            0: (0, height, ROWS),
            1: (height - OV, OV, ROWS - OV),
            -1: (0, OV, ROWS + height),
        }[di]
        column, width, column_to = {
            0: (0, breadth, LANES),
            1: (breadth - LANES, LANES, 0),
            -1: (0, LANES, LANES + breadth),
        }[dj]
        return (
            grown.at[pl.ds(ROWS + start, size), pl.ds(LANES + column, width)],
            grown.at[pl.ds(to, size), pl.ds(column_to, width)],
        )

    def field_target(di, dj):
        start, size, to = {
            0: (0, height, ROWS),
            1: (height - ROWS, ROWS, 0),
            -1: (0, ROWS, ROWS + height),
        }[di]
        if dj == 0:
            return (
                fields.at[:, pl.ds(ROWS + start, size), :], fields.at[:, pl.ds(to, size), :]
            )
        side = 0 if dj == 1 else 1
        return (pack_out.at[side, pl.ds(start, size), :], pack_in.at[side, pl.ds(to, size), :])

    def source_copy(number, di, dj):
        return copy(*source_target(di, dj), 0, number, di, dj)

    def field_copy(number, di, dj):
        return copy(*field_target(di, dj), 1, number, di, dj)

    def part_copy(turn):
        def make(number, di, dj):
            rows, columns, _, _ = part_slices(turn, di, dj, height, breadth)
            return copy(
                part.at[turn, rows, columns], arrived[turn][number], 2 + turn, number, di, dj
            )

        return make

    def start_all(make, chosen):
        for number, (di, dj) in enumerate(chosen):
            @pl.when(present(di, dj))
            def _(number=number, di=di, dj=dj):
                make(number, di, dj).start()

    def receive_all(make, chosen):
        for number, (di, dj) in enumerate(chosen):
            @pl.when(present(-di, -dj))
            def _(number=number, di=di, dj=dj):
                make(number, di, dj).wait_recv()

    def sent_all(make, chosen):
        for number, (di, dj) in enumerate(chosen):
            @pl.when(present(di, dj))
            def _(number=number, di=di, dj=dj):
                make(number, di, dj).wait_send()

    def share(turn):
        gathered[turn, me] = row_out[turn]
        to_others(
            lambda place: pltpu.make_async_remote_copy(
                src_ref=row_out.at[turn],
                dst_ref=gathered.at[turn, me],
                send_sem=row_send.at[turn],
                recv_sem=row_recv.at[turn],
                device_id=place,
                device_id_type=MESH,
            ).start()
        )

    def row_bytes(turn, sem):
        some = gathered.at[turn, pl.ds(0, devices - 1)]
        return pltpu.make_async_copy(some, some, sem.at[turn])

    def collect(turn):
        row_bytes(turn, row_recv).wait()
        return gathered[turn].reshape(devices, LANES)

    for number, (di, dj) in enumerate(directions[0]):
        @pl.when(jnp.logical_not(present(-di, -dj)))
        def _(number=number, di=di, dj=dj):
            targets = [arrived[0][number]]
            if (di, dj) in NEAR:
                targets += [
                    arrived[1][number], source_target(di, dj)[1], field_target(di, dj)[1]
                ]
            for target in targets:
                target[...] = jnp.zeros(target.shape, jnp.float32)

    unused = jnp.zeros((ROWS - OV, breadth + 2 * LANES), jnp.float32)
    grown[: ROWS - OV, :] = unused
    grown[high - ROWS + OV:, :] = unused

    loads[0].wait()
    pl.semaphore_wait(barrier, devices - 1)
    start_all(source_copy, NEAR)

    for load in loads[1:5]:
        load.wait()
    fields[1, own_rows, :] = jnp.sqrt(raw[0])
    fields[2, own_rows, :] = jnp.sqrt(raw[1])
    lane = lax.broadcasted_iota(jnp.int32, (height, LANES), 1)
    strip = LANES // 4
    to_east = jnp.zeros((height, LANES), jnp.float32)
    to_west = jnp.zeros((height, LANES), jnp.float32)
    for f in range(4):
        here = (lane >= f * strip) & (lane < (f + 1) * strip)
        east = fields[f, own_rows, breadth - LANES:]
        west = fields[f, own_rows, :LANES]
        to_east = jnp.where(here, pltpu.roll(east, ((f + 1) * strip) % LANES, 1), to_east)
        to_west = jnp.where(here, pltpu.roll(west, f * strip, 1), to_west)
    pack_out[0] = to_east
    pack_out[1] = to_west
    start_all(field_copy, NEAR)
    loads[5].wait()

    frame_row = lax.broadcasted_iota(jnp.int32, (high, wide), 0)
    frame_lane = lax.broadcasted_iota(jnp.int32, (high, wide), 1)
    grid_row = frame_row - ROWS + x * height
    grid_lane = frame_lane - SIDE + y * breadth
    inside = (
        (grid_row >= 0) & (grid_row < height * gx) & (grid_lane >= 0) & (grid_lane < breadth * gy)
    )
    own_lane = lax.broadcasted_iota(jnp.int32, (height, wide), 1)
    own = (own_lane >= SIDE) & (own_lane < SIDE + breadth)
    line_lane = lax.broadcasted_iota(jnp.int32, (lines, wide), 1)
    in_patch = (line_lane >= SIDE - OV) & (line_lane < SIDE + breadth + OV)
    vector_index = lax.broadcasted_iota(jnp.int32, (vectors, 1), 0)
    live = (vector_index < counts[0, 0]).astype(jnp.float32)
    quarter = lax.rem(me, 4)
    row_lane = lax.broadcasted_iota(jnp.int32, (1, LANES), 1)
    spot = (
        lax.broadcasted_iota(jnp.int32, (vectors, LANES), 1)
        == lax.broadcasted_iota(jnp.int32, (vectors, LANES), 0) + strip * quarter
    )
    device_row = lax.broadcasted_iota(jnp.int32, (devices, LANES), 0)
    device_lane = lax.broadcasted_iota(jnp.int32, (devices, LANES), 1)
    is_coarse = device_lane // strip == lax.rem(device_row, 4)

    def restrict():
        pieces = None
        for q in range(group):
            taken = jnp.concatenate(
                [
                    total[t, pl.ds(ROWS - OV + q, lines, stride=group), :]
                    for t in range(wide // LANES)
                ],
                axis=1,
            )
            taken = jnp.where(in_patch, taken, 0.0)
            taken = jnp.concatenate(
                [taken, jnp.zeros((lines, length - wide), jnp.float32)], axis=1
            )
            taken = pltpu.roll(taken, (py * q - (SIDE - OV)) % length, 1)
            pieces = taken if pieces is None else pieces + taken
        flat[...] = pieces
        summed = jnp.zeros((vectors, length), jnp.float32)
        for a in range(lines):
            summed = summed + basis[:, a * length:(a + 1) * length] * flat[a:a + 1, :]
        folded = summed[:, :LANES]
        for t in range(1, length // LANES):
            folded = folded + summed[:, t * LANES:(t + 1) * LANES]
        coarse = jnp.sum(folded, axis=1, keepdims=True) * live
        return jnp.sum(jnp.where(spot, coarse, 0.0), axis=0, keepdims=True)

    sublane = lax.broadcasted_iota(jnp.int32, (8, length), 0)

    def weighted(product):
        summed = product[:8]
        for k in range(8, vectors, 8):
            summed = summed + product[k:k + 8]
        return summed

    def eight_sums(pieces):
        for distance in (4, 2, 1):
            low = lax.rem(sublane // distance, 2) == 0
            merged = []
            for one, other in zip(pieces[:distance], pieces[distance:]):
                away = jnp.where(low, other, one)
                back = pltpu.roll(away, distance, 0)
                if distance != 4:
                    back = jnp.where(low, pltpu.roll(away, 8 - distance, 0), back)
                merged.append(jnp.where(low, one, other) + back)
            pieces = merged
        return pieces[0]

    def spread(rows):
        rows = jnp.where(is_coarse, rows, 0.0)
        joined = rows
        for i in range(1, 4):
            joined = joined + pltpu.roll(rows, i, 0)
        summed = jnp.zeros((vectors, LANES), jnp.float32)
        for b in range(devices // 4):
            summed = (
                summed + inverse[:, b * LANES:(b + 1) * LANES] * joined[4 * b + 3:4 * b + 4, :]
            )
        weights = jnp.sum(summed, axis=1, keepdims=True) * live
        weights = jnp.broadcast_to(weights, (vectors, LANES))
        weights = jnp.concatenate([weights] * (length // LANES), axis=1)
        whole = jnp.concatenate(
            [
                eight_sums([
                    weighted(basis[:, a * length:(a + 1) * length] * weights)
                    for a in range(first, first + 8)
                ])
                for first in range(0, lines, 8)
            ],
            axis=0,
        )
        for t in range(wide // LANES):
            total[t] = jnp.zeros((high, LANES), jnp.float32)
        for q in range(group):
            moved = pltpu.roll(whole, (SIDE - OV - py * q) % length, 1)[:, :wide]
            moved = jnp.where(in_patch, moved, 0.0)
            for t in range(wide // LANES):
                total[t, pl.ds(ROWS - OV + q, lines, stride=group), :] = (
                    moved[:, t * LANES:(t + 1) * LANES]
                )
        return get_total()

    def set_total(value):
        for t in range(wide // LANES):
            total[t] = value[:, t * LANES:(t + 1) * LANES]

    def get_total():
        return jnp.concatenate([total[t] for t in range(wide // LANES)], axis=1)

    def around(value):
        rows = value.shape[0]
        return (
            pltpu.roll(value, rows - 1, 0),
            pltpu.roll(value, 1, 0),
            pltpu.roll(value, wide - 1, 1),
            pltpu.roll(value, 1, 1),
        )

    def exchange(turn, meanwhile=lambda: None):
        start_all(part_copy(turn), directions[turn])
        set_total(part[turn])
        found = meanwhile()
        receive_all(part_copy(turn), directions[turn])
        for number, (di, dj) in enumerate(directions[turn]):
            _, _, rows, columns = part_slices(turn, di, dj, height, breadth)
            got = arrived[turn][number][...]
            first = columns.start // LANES
            for t in range(columns.size // LANES):
                total[first + t, rows, :] = (
                    total[first + t, rows, :] + got[:, t * LANES:(t + 1) * LANES]
                )
        return jnp.where(inside, get_total(), 0.0), found

    def dots(pairs, first=0):
        row = jnp.zeros((1, LANES), jnp.float32)
        place = lax.rem(quarter + 1, 4) * strip
        for i, (one, other) in enumerate(pairs):
            product = jnp.sum(jnp.where(own, one * other, 0.0), axis=0, keepdims=True)
            value = jnp.sum(product, axis=1, keepdims=True)
            row = jnp.where(row_lane == place + first + i, value, row)
        return row

    def whole_sums(rows, count):
        others = jnp.where(is_coarse, 0.0, rows)
        row = jnp.sum(others, axis=0, keepdims=True)
        return [
            jnp.sum(jnp.where(lax.rem(row_lane, strip) == i, row, 0.0), axis=1, keepdims=True)
            for i in range(count)
        ]

    receive_all(source_copy, NEAR)
    first_vector = pltpu.roll(grown[...], wide + LANES - SIDE, 1)[:, :wide]
    set_total(first_vector)
    loads[7].wait()
    row_out[0] = restrict()
    share(0)

    receive_all(field_copy, NEAR)
    patch = []
    side_lane = lax.broadcasted_iota(jnp.int32, (high, LANES), 1)
    for f in range(4):
        base = jnp.concatenate([fields[f], jnp.zeros((high, LANES), jnp.float32)], axis=1)
        base = pltpu.roll(base, SIDE, 1)
        west = pltpu.roll(pack_in[0], (SIDE - (f + 1) * strip) % LANES, 1)
        east = pltpu.roll(pack_in[1], (SIDE - f * strip) % LANES, 1)
        left = jnp.where((side_lane >= SIDE - strip) & (side_lane < SIDE), west, base[:, :LANES])
        right = jnp.where(
            (side_lane >= SIDE) & (side_lane < SIDE + strip), east, base[:, wide - LANES:]
        )
        patch.append(jnp.concatenate([left, base[:, LANES:wide - LANES], right], axis=1))
    level = jnp.exp(0.5 * patch[0])
    level_inverse = jnp.exp(-0.5 * patch[0])
    root_along, root_across = patch[1], patch[2]
    faces = (
        root_along * pltpu.roll(root_along, high - 1, 0),
        root_along * pltpu.roll(root_along, 1, 0),
        root_across * pltpu.roll(root_across, wide - 1, 1),
        root_across * pltpu.roll(root_across, 1, 1),
    )
    outflow = jnp.zeros((high, wide), jnp.float32)
    for face, beside in zip(faces, around(level_inverse)):
        outflow = outflow + face * beside
    diagonal = patch[3] + level * outflow
    diagonal = jnp.where(diagonal > 0.0, diagonal, 1.0)
    near = slice(ROWS - NARROW, ROWS + height + NARROW)
    middle = slice(NARROW, NARROW + height)
    mine = slice(ROWS, ROWS + height)
    step_size = OMEGA / diagonal[near]
    step_faces = [face[near] * step_size for face in faces]
    step_level = step_size * level[near]
    own_level_inverse = level_inverse[mine]

    def smooth(vector):
        scaled = step_level * vector[near]
        field = scaled
        for sweep in range(SWEEPS - 1):
            moved = (1.0 - OMEGA) * field + scaled
            for face, beside in zip(step_faces, around(field)):
                moved = moved + face * beside
            field = moved
        return jnp.where(own, own_level_inverse * field[middle], 0.0)

    def apply(vector, rows):
        scaled = level[rows] * vector
        image = diagonal[rows] * scaled
        for face, beside in zip(faces, around(scaled)):
            image = image - face[rows] * beside
        return level_inverse[rows] * image

    def put_part(turn, solved, spreads):
        part[turn] = spreads
        part[turn, own_rows, :] = spreads[mine] + solved

    solved = smooth(first_vector)
    loads[6].wait()
    put_part(0, solved, spread(collect(0)))
    first_dir, _ = exchange(0)
    image = apply(first_dir, slice(0, high))

    set_total(image)
    first_vector_own, image_own = first_vector[mine], image[mine]
    row_out[1] = restrict() + dots(
        [
            (first_vector_own, first_vector_own),
            (first_vector_own, image_own),
            (image_own, image_own),
        ]
    )
    share(1)
    solved = smooth(image)
    rows = collect(1)
    put_part(1, solved, spread(rows))

    def first_column():
        squares, mixed, image_squares = whole_sums(rows, 3)
        source_norm = jnp.sqrt(squares + EPSILON)
        shrink = 1.0 / source_norm
        first_first = mixed * shrink * shrink
        left_over = (
            image_squares * shrink * shrink
            - 2.0 * first_first * first_first
            + first_first * first_first * (squares * shrink * shrink)
        )
        second_first = jnp.sqrt(jnp.maximum(left_over, 0.0) + EPSILON)
        grow = 1.0 / second_first
        first = first_vector_own * shrink
        second = (image_own * shrink - first_first * first) * grow
        radius_inverse = lax.rsqrt(first_first * first_first + second_first * second_first)
        products = [(first, first), (second, second), (first, second)]
        return (
            source_norm, shrink, first_first, second_first, grow, first, second,
            radius_inverse, first_first * radius_inverse, second_first * radius_inverse,
            first_dir[near] * shrink, dots(products, 3),
        )

    second_dir, found = exchange(1, first_column)
    (
        source_norm, shrink, first_first, second_first, grow, first, second,
        radius_inverse, cosine, sine, first_dir, known_dots,
    ) = found
    second_dir = (second_dir[near] * shrink - first_first * first_dir) * grow
    image = apply(second_dir, near)[middle]
    first_dir, second_dir = first_dir[middle], second_dir[middle]
    row_out[2] = known_dots + dots([(first, image), (second, image), (image, image)])
    share(2)
    first_second, second_second, image_squares, ones, twos, cross = whole_sums(collect(2), 6)
    left_over = (
        image_squares
        - 2.0 * (first_second * first_second + second_second * second_second)
        + first_second * first_second * ones
        + second_second * second_second * twos
        + 2.0 * first_second * second_second * cross
    )
    third_square = jnp.maximum(left_over, 0.0) + EPSILON
    image = image - first_second * first - second_second * second
    upper_right = cosine * first_second + sine * second_second
    lower_right = cosine * second_second - sine * first_second
    weight_two = (
        lower_right * (-sine * source_norm) / (lower_right * lower_right + third_square)
    )
    weight_one = (cosine * source_norm - upper_right * weight_two) * radius_inverse
    remainder_one = source_norm - first_first * weight_one - first_second * weight_two
    remainder_two = -second_first * weight_one - second_second * weight_two
    answer = weight_one * first_dir + weight_two * second_dir
    remainder = remainder_one * first + remainder_two * second - weight_two * image
    both_out[0] = pltpu.roll(answer, wide - SIDE, 1)[:, :breadth]
    both_out[1] = pltpu.roll(remainder, wide - SIDE, 1)[:, :breadth]

    sent_all(source_copy, NEAR)
    sent_all(field_copy, NEAR)
    for turn in range(2):
        sent_all(part_copy(turn), directions[turn])
    for turn in range(3):
        row_bytes(turn, row_send).wait()


def on_device(
    gx, gy,
    source, potential, mobility_along, mobility_across, recombination, counts, basis, coarse_inverse
):
    height, breadth = source.shape
    vectors = basis.shape[0]
    devices = gx * gy
    high, wide = height + 2 * ROWS, breadth + 2 * SIDE
    px, py = height + 2 * OV, breadth + 2 * OV
    group = LANES // math.gcd(py, LANES)
    far = FAR if gx > 2 else []
    arrived = []
    for turn, chosen in enumerate((NEAR + far, NEAR)):
        for di, dj in chosen:
            rows, columns, _, _ = part_slices(turn, di, dj, height, breadth)
            arrived.append(pltpu.VMEM((rows.size, columns.size), jnp.float32))
    vmem = pl.BlockSpec(memory_space=pltpu.VMEM)
    hbm = pl.BlockSpec(memory_space=pltpu.HBM)
    ways = len(NEAR + far)
    both = pl.pallas_call(
        functools.partial(kernel, gx, gy, far),
        out_shape=jax.ShapeDtypeStruct((2, height, breadth), jnp.float32),
        in_specs=[hbm] * 8,
        out_specs=vmem,
        scratch_shapes=[
            pltpu.SMEM((1, 1), jnp.int32),
            pltpu.VMEM(basis.shape, jnp.float32),
            pltpu.VMEM(coarse_inverse.shape, jnp.float32),
            pltpu.VMEM((high, breadth + 2 * LANES), jnp.float32),
            pltpu.VMEM((2, height, breadth), jnp.float32),
            pltpu.VMEM((4, high, breadth), jnp.float32),
            pltpu.VMEM((2, height, LANES), jnp.float32),
            pltpu.VMEM((2, high, LANES), jnp.float32),
            pltpu.VMEM((2, high, wide), jnp.float32),
            pltpu.VMEM((wide // LANES, high, LANES), jnp.float32),
            pltpu.VMEM((px // group, py * group), jnp.float32),
            pltpu.VMEM((3, 1, LANES), jnp.float32),
            pltpu.VMEM((3, devices, 1, LANES), jnp.float32),
            *arrived,
            pltpu.SemaphoreType.DMA((8,)),
            pltpu.SemaphoreType.DMA((4, ways)),
            pltpu.SemaphoreType.DMA((4, ways)),
            pltpu.SemaphoreType.DMA((3,)),
            pltpu.SemaphoreType.DMA((3,)),
        ],
        compiler_params=pltpu.CompilerParams(
            collective_id=0, has_side_effects=True, vmem_limit_bytes=VMEM_GRANT
        ),
    )(counts, source, potential, mobility_along, mobility_across, recombination, basis, coarse_inverse)
    return both[0], both[1]


def solution(mesh):
    placed = (P("gx", "gy"),) * 7 + (P(("gx", "gy"), None),)
    return jax.shard_map(
        functools.partial(on_device, mesh.shape["gx"], mesh.shape["gy"]),
        mesh=mesh,
        in_specs=placed,
        out_specs=(P("gx", "gy"), P("gx", "gy")),
        check_vma=False,
    )
```

```python
import functools
import math
import jax
import jax.numpy as jnp
from jax import lax
from jax.experimental import pallas as pl
from jax.experimental.pallas import tpu as pltpu
from jax.sharding import PartitionSpec as P

OV = 16
SWEEPS = 8
OMEGA = 0.8
EPSILON = 1e-06
LANES = 128
ROWS = 24
SIDE = 64
FOLD = 40
FOLD_ROWS = 16
NARROW = 8
VMEM_GRANT = 63 * 1024 * 1024
MESH = pl.DeviceIdType.MESH

NEAR = [(i, j) for i in (-1, 0, 1) for j in (-1, 0, 1) if (i, j) != (0, 0)]
CORNERS = [(i, j) for i in (-1, 1) for j in (-1, 1)]
FAR = [(i, j) for i in (-2, 2) for j in (-1, 0, 1)]


def part_slices(turn, di, dj, height, breadth):
    high, wide = height + 2 * ROWS, breadth + 2 * SIDE
    margin = ROWS - OV
    reach = ROWS if turn == 0 else NARROW
    if di == 0:
        used = min(reach, OV)
        start, size, to = ROWS - used, height + 2 * used, ROWS - used
    elif di == 1:
        start, size, to = height + ROWS - reach, reach + OV, ROWS - reach
    elif di == -1:
        start, size, to = margin, reach + OV, ROWS + height - OV
    elif di == 2:
        start, size, to = 2 * height, margin, 0
    else:
        start, size, to = margin, margin, high - margin
    if dj == 0:
        lane, width, lane_to = 0, wide, 0
    elif dj == 1:
        lane, width, lane_to = wide - LANES, LANES, 0
    else:
        lane, width, lane_to = 0, LANES, wide - LANES
    return (pl.ds(start, size), pl.ds(lane, width), pl.ds(to, size), pl.ds(lane_to, width))


def kernel(
    gx, gy, far,
    counts_hbm, source, potential, along, across, recombination, basis_hbm, inverse_hbm,
    both_out,
    counts, basis, inverse, grown, raw, fields, pack_out, pack_in, part, corners, total, flat, row_out,
    gathered, *rest,
):
    directions = (NEAR + far, NEAR)
    arrived = (rest[: len(directions[0])], rest[len(directions[0]):][: len(NEAR)])
    load_sem, send_sem, recv_sem, row_send, row_recv = rest[len(directions[0]) + len(NEAR):]
    devices = gx * gy
    x = lax.axis_index("gx")
    y = lax.axis_index("gy")
    me = x * gy + y
    height, breadth = source.shape
    vectors = basis.shape[0]
    high, wide = height + 2 * ROWS, breadth + 2 * SIDE
    px, py = height + 2 * OV, breadth + 2 * OV
    group = LANES // math.gcd(py, LANES)
    lines, length = px // group, py * group
    own_rows = pl.ds(ROWS, height)

    def wrapped(place, step, size):
        return jnp.where(place + step >= size, place + step - size, place + step)

    few = devices <= 64
    along_x = [wrapped(x, a, gx) if a else x for a in range(gx)]
    along_y = [wrapped(y, b, gy) if b else y for b in range(gy)] if few else []

    def to_others(act):
        for a in reversed(range(gx)):
            if few:
                for b in sorted(range(gy), key=lambda b: abs(2 * b - gy)):
                    if a or b:
                        act((along_x[a], along_y[b]))
            else:
                def step(b, carry, a=a):
                    act((along_x[a], wrapped(y, b, gy)))
                    return carry

                lax.fori_loop(0 if a else 1, gy, step, 0)

    sources = [
        (source, grown.at[own_rows, pl.ds(LANES, breadth)]),
        (potential, fields.at[0, own_rows, :]),
        (along, raw.at[0]),
        (across, raw.at[1]),
        (recombination, fields.at[3, own_rows, :]),
        (counts_hbm, counts),
        (inverse_hbm, inverse),
        (basis_hbm, basis),
    ]
    loads = [
        pltpu.make_async_copy(src, dst, load_sem.at[i]) for i, (src, dst) in enumerate(sources)
    ]
    for load in loads:
        load.start()
    barrier = pltpu.get_barrier_semaphore()
    to_others(
        lambda place: pl.semaphore_signal(barrier, inc=1, device_id=place, device_id_type=MESH)
    )

    def present(di, dj):
        return (x + di >= 0) & (x + di < gx) & (y + dj >= 0) & (y + dj < gy)

    def copy(src, dst, phase, number, di, dj):
        return pltpu.make_async_remote_copy(
            src_ref=src,
            dst_ref=dst,
            send_sem=send_sem.at[phase, number],
            recv_sem=recv_sem.at[phase, number],
            device_id=(x + di, y + dj),
            device_id_type=MESH,
        )

    def source_target(di, dj):
        start, size, to = {
            0: (0, height, ROWS),
            1: (height - OV, OV, ROWS - OV),
            -1: (0, OV, ROWS + height),
        }[di]
        column, width, column_to = {
            0: (0, breadth, LANES),
            1: (breadth - LANES, LANES, 0),
            -1: (0, LANES, LANES + breadth),
        }[dj]
        return (
            grown.at[pl.ds(ROWS + start, size), pl.ds(LANES + column, width)],
            grown.at[pl.ds(to, size), pl.ds(column_to, width)],
        )

    def field_target(di, dj):
        start, size, to = {
            0: (0, height, ROWS),
            1: (height - ROWS, ROWS, 0),
            -1: (0, ROWS, ROWS + height),
        }[di]
        if dj == 0:
            return (
                fields.at[:, pl.ds(ROWS + start, size), :], fields.at[:, pl.ds(to, size), :]
            )
        side = 0 if dj == 1 else 1
        return (pack_out.at[side, pl.ds(start, size), :], pack_in.at[side, pl.ds(to, size), :])

    def source_copy(number, di, dj):
        return copy(*source_target(di, dj), 0, number, di, dj)

    def field_copy(number, di, dj):
        return copy(*field_target(di, dj), 1, number, di, dj)

    def part_copy(turn):
        def make(number, di, dj):
            rows, columns, _, _ = part_slices(turn, di, dj, height, breadth)
            src = part.at[turn, rows, columns]
            if (di, dj) in CORNERS:
                src = corners.at[turn, CORNERS.index((di, dj))]
            return copy(src, arrived[turn][number], 2 + turn, number, di, dj)

        return make

    def start_all(make, chosen, corner=None):
        for number, (di, dj) in enumerate(chosen):
            if corner is not None and corner != ((di, dj) in CORNERS):
                continue

            @pl.when(present(di, dj))
            def _(number=number, di=di, dj=dj):
                make(number, di, dj).start()

    def receive_all(make, chosen):
        for number, (di, dj) in enumerate(chosen):
            @pl.when(present(-di, -dj))
            def _(number=number, di=di, dj=dj):
                make(number, di, dj).wait_recv()

    def sent_all(make, chosen):
        for number, (di, dj) in enumerate(chosen):
            @pl.when(present(di, dj))
            def _(number=number, di=di, dj=dj):
                make(number, di, dj).wait_send()

    def share(turn):
        gathered[turn, me] = row_out[turn]
        to_others(
            lambda place: pltpu.make_async_remote_copy(
                src_ref=row_out.at[turn],
                dst_ref=gathered.at[turn, me],
                send_sem=row_send.at[turn],
                recv_sem=row_recv.at[turn],
                device_id=place,
                device_id_type=MESH,
            ).start()
        )

    def row_bytes(turn, sem):
        some = gathered.at[turn, pl.ds(0, devices - 1)]
        return pltpu.make_async_copy(some, some, sem.at[turn])

    def collect(turn):
        row_bytes(turn, row_recv).wait()
        return gathered[turn].reshape(devices, LANES)

    for number, (di, dj) in enumerate(directions[0]):
        @pl.when(jnp.logical_not(present(-di, -dj)))
        def _(number=number, di=di, dj=dj):
            targets = [arrived[0][number]]
            if (di, dj) in NEAR:
                targets += [
                    arrived[1][number], source_target(di, dj)[1], field_target(di, dj)[1]
                ]
            for target in targets:
                target[...] = jnp.zeros(target.shape, jnp.float32)

    unused = jnp.zeros((ROWS - OV, breadth + 2 * LANES), jnp.float32)
    grown[: ROWS - OV, :] = unused
    grown[high - ROWS + OV:, :] = unused

    loads[0].wait()
    pl.semaphore_wait(barrier, devices - 1)
    start_all(source_copy, NEAR)

    for load in loads[1:5]:
        load.wait()
    fields[1, own_rows, :] = jnp.sqrt(raw[0])
    fields[2, own_rows, :] = jnp.sqrt(raw[1])
    lane = lax.broadcasted_iota(jnp.int32, (height, LANES), 1)
    strip = LANES // 4
    to_east = jnp.zeros((height, LANES), jnp.float32)
    to_west = jnp.zeros((height, LANES), jnp.float32)
    for f in range(4):
        here = (lane >= f * strip) & (lane < (f + 1) * strip)
        east = fields[f, own_rows, breadth - LANES:]
        west = fields[f, own_rows, :LANES]
        to_east = jnp.where(here, pltpu.roll(east, ((f + 1) * strip) % LANES, 1), to_east)
        to_west = jnp.where(here, pltpu.roll(west, f * strip, 1), to_west)
    pack_out[0] = to_east
    pack_out[1] = to_west
    start_all(field_copy, NEAR)
    loads[5].wait()

    frame_row = lax.broadcasted_iota(jnp.int32, (high, wide), 0)
    frame_lane = lax.broadcasted_iota(jnp.int32, (high, wide), 1)
    grid_row = frame_row - ROWS + x * height
    grid_lane = frame_lane - SIDE + y * breadth
    inside = (
        (grid_row >= 0) & (grid_row < height * gx) & (grid_lane >= 0) & (grid_lane < breadth * gy)
    )
    own_lane = lax.broadcasted_iota(jnp.int32, (height, wide), 1)
    own = (own_lane >= SIDE) & (own_lane < SIDE + breadth)
    line_lane = lax.broadcasted_iota(jnp.int32, (lines, wide), 1)
    in_patch = (line_lane >= SIDE - OV) & (line_lane < SIDE + breadth + OV)
    vector_index = lax.broadcasted_iota(jnp.int32, (vectors, 1), 0)
    live = (vector_index < counts[0, 0]).astype(jnp.float32)
    quarter = lax.rem(me, 4)
    row_lane = lax.broadcasted_iota(jnp.int32, (1, LANES), 1)
    spot = (
        lax.broadcasted_iota(jnp.int32, (vectors, LANES), 1)
        == lax.broadcasted_iota(jnp.int32, (vectors, LANES), 0) + strip * quarter
    )
    device_row = lax.broadcasted_iota(jnp.int32, (devices, LANES), 0)
    device_lane = lax.broadcasted_iota(jnp.int32, (devices, LANES), 1)
    is_coarse = device_lane // strip == lax.rem(device_row, 4)

    def restrict():
        pieces = None
        for q in range(group):
            taken = jnp.concatenate(
                [
                    total[t, pl.ds(ROWS - OV + q, lines, stride=group), :]
                    for t in range(wide // LANES)
                ],
                axis=1,
            )
            taken = jnp.where(in_patch, taken, 0.0)
            taken = jnp.concatenate(
                [taken, jnp.zeros((lines, length - wide), jnp.float32)], axis=1
            )
            taken = pltpu.roll(taken, (py * q - (SIDE - OV)) % length, 1)
            pieces = taken if pieces is None else pieces + taken
        flat[...] = pieces
        summed = jnp.zeros((vectors, length), jnp.float32)
        for a in range(lines):
            summed = summed + basis[:, a * length:(a + 1) * length] * flat[a:a + 1, :]
        folded = summed[:, :LANES]
        for t in range(1, length // LANES):
            folded = folded + summed[:, t * LANES:(t + 1) * LANES]
        coarse = jnp.sum(folded, axis=1, keepdims=True) * live
        return jnp.sum(jnp.where(spot, coarse, 0.0), axis=0, keepdims=True)

    sublane = lax.broadcasted_iota(jnp.int32, (8, length), 0)

    def weighted(product):
        summed = product[:8]
        for k in range(8, vectors, 8):
            summed = summed + product[k:k + 8]
        return summed

    def eight_sums(pieces):
        for distance in (4, 2, 1):
            low = lax.rem(sublane // distance, 2) == 0
            merged = []
            for one, other in zip(pieces[:distance], pieces[distance:]):
                away = jnp.where(low, other, one)
                back = pltpu.roll(away, distance, 0)
                if distance != 4:
                    back = jnp.where(low, pltpu.roll(away, 8 - distance, 0), back)
                merged.append(jnp.where(low, one, other) + back)
            pieces = merged
        return pieces[0]

    def spread(rows):
        rows = jnp.where(is_coarse, rows, 0.0)
        joined = rows
        for i in range(1, 4):
            joined = joined + pltpu.roll(rows, i, 0)
        summed = jnp.zeros((vectors, LANES), jnp.float32)
        for b in range(devices // 4):
            summed = (
                summed + inverse[:, b * LANES:(b + 1) * LANES] * joined[4 * b + 3:4 * b + 4, :]
            )
        weights = jnp.sum(summed, axis=1, keepdims=True) * live
        weights = jnp.broadcast_to(weights, (vectors, LANES))
        weights = jnp.concatenate([weights] * (length // LANES), axis=1)
        whole = jnp.concatenate(
            [
                eight_sums([
                    weighted(basis[:, a * length:(a + 1) * length] * weights)
                    for a in range(first, first + 8)
                ])
                for first in range(0, lines, 8)
            ],
            axis=0,
        )
        for t in range(wide // LANES):
            total[t] = jnp.zeros((high, LANES), jnp.float32)
        for q in range(group):
            moved = pltpu.roll(whole, (SIDE - OV - py * q) % length, 1)[:, :wide]
            moved = jnp.where(in_patch, moved, 0.0)
            for t in range(wide // LANES):
                total[t, pl.ds(ROWS - OV + q, lines, stride=group), :] = (
                    moved[:, t * LANES:(t + 1) * LANES]
                )
        return get_total()

    def set_total(value):
        for t in range(wide // LANES):
            total[t] = value[:, t * LANES:(t + 1) * LANES]

    def get_total():
        return jnp.concatenate([total[t] for t in range(wide // LANES)], axis=1)

    def around(value):
        rows = value.shape[0]
        return (
            pltpu.roll(value, rows - 1, 0),
            pltpu.roll(value, 1, 0),
            pltpu.roll(value, wide - 1, 1),
            pltpu.roll(value, 1, 1),
        )

    fold_lane = SIDE - OV - 4
    fold_lanes = lax.broadcasted_iota(jnp.int32, (FOLD_ROWS, LANES), 1)
    fold_place = fold_lanes // FOLD
    in_fold = (fold_lanes >= fold_lane) & (fold_lanes < fold_lane + FOLD)

    def folds(di):
        away = [height + i * FOLD_ROWS for i in range(3)]
        near_rows = [i * FOLD_ROWS for i in range(3)]
        return (away, near_rows) if di == 1 else (near_rows, away)

    def exchange(turn, meanwhile=lambda: None):
        start_all(part_copy(turn), directions[turn], corner=False)
        for number, (di, dj) in enumerate(CORNERS):
            side = part[turn, :, wide - LANES:] if dj == 1 else part[turn, :, :LANES]
            folded = jnp.zeros((FOLD_ROWS, LANES), jnp.float32)
            for strip_number, row in enumerate(folds(di)[0]):
                moved = pltpu.roll(
                    side[row:row + FOLD_ROWS], (FOLD * strip_number - fold_lane) % LANES, 1
                )
                folded = jnp.where(fold_place == strip_number, moved, folded)
            corners[turn, number] = folded
        start_all(part_copy(turn), directions[turn], corner=True)
        set_total(part[turn])
        found = meanwhile()
        receive_all(part_copy(turn), directions[turn])
        for number, (di, dj) in enumerate(directions[turn]):
            _, _, rows, columns = part_slices(turn, di, dj, height, breadth)
            got = arrived[turn][number][...]
            first = columns.start // LANES
            if (di, dj) in CORNERS:
                for strip_number, row in enumerate(folds(di)[1]):
                    moved = pltpu.roll(got, (fold_lane - FOLD * strip_number) % LANES, 1)
                    moved = jnp.where(in_fold, moved, 0.0)
                    at = pl.ds(row, FOLD_ROWS)
                    total[first, at, :] = total[first, at, :] + moved
                continue
            for t in range(columns.size // LANES):
                total[first + t, rows, :] = (
                    total[first + t, rows, :] + got[:, t * LANES:(t + 1) * LANES]
                )
        return jnp.where(inside, get_total(), 0.0), found

    def dots(pairs, first=0):
        row = jnp.zeros((1, LANES), jnp.float32)
        place = lax.rem(quarter + 1, 4) * strip
        for i, (one, other) in enumerate(pairs):
            product = jnp.sum(jnp.where(own, one * other, 0.0), axis=0, keepdims=True)
            value = jnp.sum(product, axis=1, keepdims=True)
            row = jnp.where(row_lane == place + first + i, value, row)
        return row

    def whole_sums(rows, count):
        others = jnp.where(is_coarse, 0.0, rows)
        row = jnp.sum(others, axis=0, keepdims=True)
        return [
            jnp.sum(jnp.where(lax.rem(row_lane, strip) == i, row, 0.0), axis=1, keepdims=True)
            for i in range(count)
        ]

    receive_all(source_copy, NEAR)
    first_vector = pltpu.roll(grown[...], wide + LANES - SIDE, 1)[:, :wide]
    set_total(first_vector)
    loads[7].wait()
    row_out[0] = restrict()
    share(0)

    receive_all(field_copy, NEAR)
    patch = []
    side_lane = lax.broadcasted_iota(jnp.int32, (high, LANES), 1)
    for f in range(4):
        base = jnp.concatenate([fields[f], jnp.zeros((high, LANES), jnp.float32)], axis=1)
        base = pltpu.roll(base, SIDE, 1)
        west = pltpu.roll(pack_in[0], (SIDE - (f + 1) * strip) % LANES, 1)
        east = pltpu.roll(pack_in[1], (SIDE - f * strip) % LANES, 1)
        left = jnp.where((side_lane >= SIDE - strip) & (side_lane < SIDE), west, base[:, :LANES])
        right = jnp.where(
            (side_lane >= SIDE) & (side_lane < SIDE + strip), east, base[:, wide - LANES:]
        )
        patch.append(jnp.concatenate([left, base[:, LANES:wide - LANES], right], axis=1))
    level = jnp.exp(0.5 * patch[0])
    level_inverse = jnp.exp(-0.5 * patch[0])
    root_along, root_across = patch[1], patch[2]
    faces = (
        root_along * pltpu.roll(root_along, high - 1, 0),
        root_along * pltpu.roll(root_along, 1, 0),
        root_across * pltpu.roll(root_across, wide - 1, 1),
        root_across * pltpu.roll(root_across, 1, 1),
    )
    outflow = jnp.zeros((high, wide), jnp.float32)
    for face, beside in zip(faces, around(level_inverse)):
        outflow = outflow + face * beside
    diagonal = patch[3] + level * outflow
    diagonal = jnp.where(diagonal > 0.0, diagonal, 1.0)
    near = slice(ROWS - NARROW, ROWS + height + NARROW)
    middle = slice(NARROW, NARROW + height)
    mine = slice(ROWS, ROWS + height)
    step_size = OMEGA / diagonal[near]
    step_faces = [face[near] * step_size for face in faces]
    step_level = step_size * level[near]
    own_level_inverse = level_inverse[mine]

    def smooth(vector):
        scaled = step_level * vector[near]
        field = scaled
        for sweep in range(SWEEPS - 1):
            moved = (1.0 - OMEGA) * field + scaled
            for face, beside in zip(step_faces, around(field)):
                moved = moved + face * beside
            field = moved
        return jnp.where(own, own_level_inverse * field[middle], 0.0)

    def apply(vector, rows):
        scaled = level[rows] * vector
        image = diagonal[rows] * scaled
        for face, beside in zip(faces, around(scaled)):
            image = image - face[rows] * beside
        return level_inverse[rows] * image

    def put_part(turn, solved, spreads):
        part[turn] = spreads
        part[turn, own_rows, :] = spreads[mine] + solved

    solved = smooth(first_vector)
    loads[6].wait()
    put_part(0, solved, spread(collect(0)))
    first_dir, _ = exchange(0)
    image = apply(first_dir, slice(0, high))

    set_total(image)
    first_vector_own, image_own = first_vector[mine], image[mine]
    row_out[1] = restrict() + dots(
        [
            (first_vector_own, first_vector_own),
            (first_vector_own, image_own),
            (image_own, image_own),
        ]
    )
    share(1)
    solved = smooth(image)
    rows = collect(1)
    put_part(1, solved, spread(rows))

    def first_column():
        squares, mixed, image_squares = whole_sums(rows, 3)
        source_norm = jnp.sqrt(squares + EPSILON)
        shrink = 1.0 / source_norm
        first_first = mixed * shrink * shrink
        left_over = (
            image_squares * shrink * shrink
            - 2.0 * first_first * first_first
            + first_first * first_first * (squares * shrink * shrink)
        )
        second_first = jnp.sqrt(jnp.maximum(left_over, 0.0) + EPSILON)
        grow = 1.0 / second_first
        first = first_vector_own * shrink
        second = (image_own * shrink - first_first * first) * grow
        radius_inverse = lax.rsqrt(first_first * first_first + second_first * second_first)
        products = [(first, first), (second, second), (first, second)]
        return (
            source_norm, shrink, first_first, second_first, grow, first, second,
            radius_inverse, first_first * radius_inverse, second_first * radius_inverse,
            first_dir[near] * shrink, dots(products, 3),
        )

    second_dir, found = exchange(1, first_column)
    (
        source_norm, shrink, first_first, second_first, grow, first, second,
        radius_inverse, cosine, sine, first_dir, known_dots,
    ) = found
    second_dir = (second_dir[near] * shrink - first_first * first_dir) * grow
    image = apply(second_dir, near)[middle]
    first_dir, second_dir = first_dir[middle], second_dir[middle]
    row_out[2] = known_dots + dots([(first, image), (second, image), (image, image)])
    share(2)
    sent_all(source_copy, NEAR)
    sent_all(field_copy, NEAR)
    for turn in range(2):
        sent_all(part_copy(turn), directions[turn])
        row_bytes(turn, row_send).wait()
    first_second, second_second, image_squares, ones, twos, cross = whole_sums(collect(2), 6)
    left_over = (
        image_squares
        - 2.0 * (first_second * first_second + second_second * second_second)
        + first_second * first_second * ones
        + second_second * second_second * twos
        + 2.0 * first_second * second_second * cross
    )
    third_square = jnp.maximum(left_over, 0.0) + EPSILON
    image = image - first_second * first - second_second * second
    upper_right = cosine * first_second + sine * second_second
    lower_right = cosine * second_second - sine * first_second
    weight_two = (
        lower_right * (-sine * source_norm) / (lower_right * lower_right + third_square)
    )
    weight_one = (cosine * source_norm - upper_right * weight_two) * radius_inverse
    remainder_one = source_norm - first_first * weight_one - first_second * weight_two
    remainder_two = -second_first * weight_one - second_second * weight_two
    answer = weight_one * first_dir + weight_two * second_dir
    remainder = remainder_one * first + remainder_two * second - weight_two * image
    both_out[0] = pltpu.roll(answer, wide - SIDE, 1)[:, :breadth]
    both_out[1] = pltpu.roll(remainder, wide - SIDE, 1)[:, :breadth]
    row_bytes(2, row_send).wait()


def on_device(
    gx, gy,
    source, potential, mobility_along, mobility_across, recombination, counts, basis, coarse_inverse
):
    height, breadth = source.shape
    vectors = basis.shape[0]
    devices = gx * gy
    high, wide = height + 2 * ROWS, breadth + 2 * SIDE
    px, py = height + 2 * OV, breadth + 2 * OV
    group = LANES // math.gcd(py, LANES)
    far = FAR if gx > 2 else []
    arrived = []
    for turn, chosen in enumerate((NEAR + far, NEAR)):
        for di, dj in chosen:
            rows, columns, _, _ = part_slices(turn, di, dj, height, breadth)
            shape = (rows.size, columns.size)
            if (di, dj) in CORNERS:
                shape = (FOLD_ROWS, LANES)
            arrived.append(pltpu.VMEM(shape, jnp.float32))
    vmem = pl.BlockSpec(memory_space=pltpu.VMEM)
    hbm = pl.BlockSpec(memory_space=pltpu.HBM)
    ways = len(NEAR + far)
    both = pl.pallas_call(
        functools.partial(kernel, gx, gy, far),
        out_shape=jax.ShapeDtypeStruct((2, height, breadth), jnp.float32),
        in_specs=[hbm] * 8,
        out_specs=vmem,
        scratch_shapes=[
            pltpu.SMEM((1, 1), jnp.int32),
            pltpu.VMEM(basis.shape, jnp.float32),
            pltpu.VMEM(coarse_inverse.shape, jnp.float32),
            pltpu.VMEM((high, breadth + 2 * LANES), jnp.float32),
            pltpu.VMEM((2, height, breadth), jnp.float32),
            pltpu.VMEM((4, high, breadth), jnp.float32),
            pltpu.VMEM((2, height, LANES), jnp.float32),
            pltpu.VMEM((2, high, LANES), jnp.float32),
            pltpu.VMEM((2, high, wide), jnp.float32),
            pltpu.VMEM((2, len(CORNERS), FOLD_ROWS, LANES), jnp.float32),
            pltpu.VMEM((wide // LANES, high, LANES), jnp.float32),
            pltpu.VMEM((px // group, py * group), jnp.float32),
            pltpu.VMEM((3, 1, LANES), jnp.float32),
            pltpu.VMEM((3, devices, 1, LANES), jnp.float32),
            *arrived,
            pltpu.SemaphoreType.DMA((8,)),
            pltpu.SemaphoreType.DMA((4, ways)),
            pltpu.SemaphoreType.DMA((4, ways)),
            pltpu.SemaphoreType.DMA((3,)),
            pltpu.SemaphoreType.DMA((3,)),
        ],
        compiler_params=pltpu.CompilerParams(
            collective_id=0, has_side_effects=True, vmem_limit_bytes=VMEM_GRANT
        ),
    )(counts, source, potential, mobility_along, mobility_across, recombination, basis, coarse_inverse)
    return both[0], both[1]


def solution(mesh):
    placed = (P("gx", "gy"),) * 7 + (P(("gx", "gy"), None),)
    return jax.shard_map(
        functools.partial(on_device, mesh.shape["gx"], mesh.shape["gy"]),
        mesh=mesh,
        in_specs=placed,
        out_specs=(P("gx", "gy"), P("gx", "gy")),
        check_vma=False,
    )
```

```python
import functools
import math
import jax
import jax.numpy as jnp
from jax import lax
from jax.experimental import pallas as pl
from jax.experimental.pallas import tpu as pltpu
from jax.sharding import PartitionSpec as P

OV = 16
SWEEPS = 8
OMEGA = 0.8
EPSILON = 1e-06
LANES = 128
ROWS = 24
SIDE = 64
FOLD = 40
FOLD_ROWS = 16
NARROW = 8
VMEM_GRANT = 63 * 1024 * 1024
MESH = pl.DeviceIdType.MESH

NEAR = [(i, j) for i in (-1, 0, 1) for j in (-1, 0, 1) if (i, j) != (0, 0)]
UPRIGHT = [(-1, 0), (1, 0)]
CORNERS = [(i, j) for i in (-1, 1) for j in (-1, 1)]
FAR = [(i, j) for i in (-2, 2) for j in (-1, 0, 1)]


def part_slices(turn, di, dj, height, breadth):
    high, wide = height + 2 * ROWS, breadth + 2 * SIDE
    margin = ROWS - OV
    reach = ROWS if turn == 0 else NARROW
    if di == 0:
        used = min(reach, OV)
        start, size, to = ROWS - used, height + 2 * used, ROWS - used
    elif di == 1:
        start, size, to = height + ROWS - reach, reach + OV, ROWS - reach
    elif di == -1:
        start, size, to = margin, reach + OV, ROWS + height - OV
    elif di == 2:
        start, size, to = 2 * height, margin, 0
    else:
        start, size, to = margin, margin, high - margin
    if dj == 0:
        lane, width, lane_to = 0, wide, 0
    elif dj == 1:
        lane, width, lane_to = wide - LANES, LANES, 0
    else:
        lane, width, lane_to = 0, LANES, wide - LANES
    return (pl.ds(start, size), pl.ds(lane, width), pl.ds(to, size), pl.ds(lane_to, width))


def kernel(
    gx, gy, far,
    counts_hbm, source, potential, along, across, recombination, basis_hbm, inverse_hbm,
    both_out,
    counts, basis, inverse, grown, raw, fields, pack_out, pack_in, part, corners, total, flat, row_out,
    gathered, *rest,
):
    directions = (NEAR + far, NEAR)
    arrived = (rest[: len(directions[0])], rest[len(directions[0]):][: len(NEAR)])
    load_sem, send_sem, recv_sem, row_send, row_recv = rest[len(directions[0]) + len(NEAR):]
    devices = gx * gy
    x = lax.axis_index("gx")
    y = lax.axis_index("gy")
    me = x * gy + y
    height, breadth = source.shape
    vectors = basis.shape[0]
    high, wide = height + 2 * ROWS, breadth + 2 * SIDE
    px, py = height + 2 * OV, breadth + 2 * OV
    group = LANES // math.gcd(py, LANES)
    lines, length = px // group, py * group
    own_rows = pl.ds(ROWS, height)

    def wrapped(place, step, size):
        return jnp.where(place + step >= size, place + step - size, place + step)

    few = devices <= 64
    along_x = [wrapped(x, a, gx) if a else x for a in range(gx)]
    along_y = [wrapped(y, b, gy) if b else y for b in range(gy)] if few else []

    def to_others(act):
        for a in reversed(range(gx)):
            if few:
                for b in sorted(range(gy), key=lambda b: abs(2 * b - gy)):
                    if a or b:
                        act((along_x[a], along_y[b]))
            else:
                def step(b, carry, a=a):
                    act((along_x[a], wrapped(y, b, gy)))
                    return carry

                lax.fori_loop(0 if a else 1, gy, step, 0)

    sources = [
        (source, grown.at[own_rows, pl.ds(LANES, breadth)]),
        (potential, fields.at[0, own_rows, :]),
        (along, raw.at[0]),
        (across, raw.at[1]),
        (recombination, fields.at[3, own_rows, :]),
        (counts_hbm, counts),
        (inverse_hbm, inverse),
        (basis_hbm, basis),
    ]
    loads = [
        pltpu.make_async_copy(src, dst, load_sem.at[i]) for i, (src, dst) in enumerate(sources)
    ]
    for load in loads:
        load.start()
    barrier = pltpu.get_barrier_semaphore()
    to_others(
        lambda place: pl.semaphore_signal(barrier, inc=1, device_id=place, device_id_type=MESH)
    )

    def present(di, dj):
        return (x + di >= 0) & (x + di < gx) & (y + dj >= 0) & (y + dj < gy)

    def copy(src, dst, phase, number, di, dj):
        return pltpu.make_async_remote_copy(
            src_ref=src,
            dst_ref=dst,
            send_sem=send_sem.at[phase, number],
            recv_sem=recv_sem.at[phase, number],
            device_id=(x + di, y + dj),
            device_id_type=MESH,
        )

    def source_target(di, dj):
        start, size, to = {
            0: (0, height, ROWS),
            1: (height - OV, OV, ROWS - OV),
            -1: (0, OV, ROWS + height),
        }[di]
        column, width, column_to = {
            0: (0, breadth, LANES),
            1: (breadth - LANES, LANES, 0),
            -1: (0, LANES, LANES + breadth),
        }[dj]
        return (
            grown.at[pl.ds(ROWS + start, size), pl.ds(LANES + column, width)],
            grown.at[pl.ds(to, size), pl.ds(column_to, width)],
        )

    def field_target(di, dj, later=False):
        start, size, to = {
            0: (0, height, ROWS),
            1: (height - ROWS, ROWS, 0),
            -1: (0, ROWS, ROWS + height),
        }[di]
        if dj == 0:
            if later:
                size = ROWS - NARROW
                if di == -1:
                    start, to = start + NARROW, to + NARROW
            else:
                size = NARROW
                if di == 1:
                    start, to = start + ROWS - NARROW, to + ROWS - NARROW
            return (
                fields.at[:, pl.ds(ROWS + start, size), :], fields.at[:, pl.ds(to, size), :]
            )
        side = 0 if dj == 1 else 1
        return (pack_out.at[side, pl.ds(start, size), :], pack_in.at[side, pl.ds(to, size), :])

    def source_copy(number, di, dj):
        return copy(*source_target(di, dj), 0, number, di, dj)

    def field_copy(number, di, dj):
        return copy(*field_target(di, dj), 1, number, di, dj)

    def later_copy(number, di, dj):
        return copy(*field_target(di, dj, True), 4, number, di, dj)

    def part_copy(turn):
        def make(number, di, dj):
            rows, columns, _, _ = part_slices(turn, di, dj, height, breadth)
            src = part.at[turn, rows, columns]
            if (di, dj) in CORNERS:
                src = corners.at[turn, CORNERS.index((di, dj))]
            return copy(src, arrived[turn][number], 2 + turn, number, di, dj)

        return make

    def start_all(make, chosen, corner=None):
        for number, (di, dj) in enumerate(chosen):
            if corner is not None and corner != ((di, dj) in CORNERS):
                continue

            @pl.when(present(di, dj))
            def _(number=number, di=di, dj=dj):
                make(number, di, dj).start()

    def receive_all(make, chosen):
        for number, (di, dj) in enumerate(chosen):
            @pl.when(present(-di, -dj))
            def _(number=number, di=di, dj=dj):
                make(number, di, dj).wait_recv()

    def sent_all(make, chosen):
        for number, (di, dj) in enumerate(chosen):
            @pl.when(present(di, dj))
            def _(number=number, di=di, dj=dj):
                make(number, di, dj).wait_send()

    def share(turn):
        gathered[turn, me] = row_out[turn]
        to_others(
            lambda place: pltpu.make_async_remote_copy(
                src_ref=row_out.at[turn],
                dst_ref=gathered.at[turn, me],
                send_sem=row_send.at[turn],
                recv_sem=row_recv.at[turn],
                device_id=place,
                device_id_type=MESH,
            ).start()
        )

    def row_bytes(turn, sem):
        some = gathered.at[turn, pl.ds(0, devices - 1)]
        return pltpu.make_async_copy(some, some, sem.at[turn])

    def collect(turn):
        row_bytes(turn, row_recv).wait()
        return gathered[turn].reshape(devices, LANES)

    for number, (di, dj) in enumerate(directions[0]):
        @pl.when(jnp.logical_not(present(-di, -dj)))
        def _(number=number, di=di, dj=dj):
            targets = [arrived[0][number]]
            if (di, dj) in NEAR:
                targets += [
                    arrived[1][number], source_target(di, dj)[1], field_target(di, dj)[1]
                ]
            if (di, dj) in UPRIGHT:
                targets.append(field_target(di, dj, True)[1])
            for target in targets:
                target[...] = jnp.zeros(target.shape, jnp.float32)

    unused = jnp.zeros((ROWS - OV, breadth + 2 * LANES), jnp.float32)
    grown[: ROWS - OV, :] = unused
    grown[high - ROWS + OV:, :] = unused

    loads[0].wait()
    pl.semaphore_wait(barrier, devices - 1)
    start_all(source_copy, NEAR)

    for load in loads[1:5]:
        load.wait()
    fields[1, own_rows, :] = jnp.sqrt(raw[0])
    fields[2, own_rows, :] = jnp.sqrt(raw[1])
    lane = lax.broadcasted_iota(jnp.int32, (height, LANES), 1)
    strip = LANES // 4
    to_east = jnp.zeros((height, LANES), jnp.float32)
    to_west = jnp.zeros((height, LANES), jnp.float32)
    for f in range(4):
        here = (lane >= f * strip) & (lane < (f + 1) * strip)
        east = fields[f, own_rows, breadth - LANES:]
        west = fields[f, own_rows, :LANES]
        to_east = jnp.where(here, pltpu.roll(east, ((f + 1) * strip) % LANES, 1), to_east)
        to_west = jnp.where(here, pltpu.roll(west, f * strip, 1), to_west)
    pack_out[0] = to_east
    pack_out[1] = to_west
    start_all(field_copy, NEAR)
    start_all(later_copy, UPRIGHT)
    loads[5].wait()

    frame_row = lax.broadcasted_iota(jnp.int32, (high, wide), 0)
    frame_lane = lax.broadcasted_iota(jnp.int32, (high, wide), 1)
    grid_row = frame_row - ROWS + x * height
    grid_lane = frame_lane - SIDE + y * breadth
    inside = (
        (grid_row >= 0) & (grid_row < height * gx) & (grid_lane >= 0) & (grid_lane < breadth * gy)
    )
    own_lane = lax.broadcasted_iota(jnp.int32, (height, wide), 1)
    own = (own_lane >= SIDE) & (own_lane < SIDE + breadth)
    line_lane = lax.broadcasted_iota(jnp.int32, (lines, wide), 1)
    in_patch = (line_lane >= SIDE - OV) & (line_lane < SIDE + breadth + OV)
    vector_index = lax.broadcasted_iota(jnp.int32, (vectors, 1), 0)
    live = (vector_index < counts[0, 0]).astype(jnp.float32)
    quarter = lax.rem(me, 4)
    row_lane = lax.broadcasted_iota(jnp.int32, (1, LANES), 1)
    spot = (
        lax.broadcasted_iota(jnp.int32, (vectors, LANES), 1)
        == lax.broadcasted_iota(jnp.int32, (vectors, LANES), 0) + strip * quarter
    )
    device_row = lax.broadcasted_iota(jnp.int32, (devices, LANES), 0)
    device_lane = lax.broadcasted_iota(jnp.int32, (devices, LANES), 1)
    is_coarse = device_lane // strip == lax.rem(device_row, 4)

    def restrict():
        pieces = None
        for q in range(group):
            taken = jnp.concatenate(
                [
                    total[t, pl.ds(ROWS - OV + q, lines, stride=group), :]
                    for t in range(wide // LANES)
                ],
                axis=1,
            )
            taken = jnp.where(in_patch, taken, 0.0)
            taken = jnp.concatenate(
                [taken, jnp.zeros((lines, length - wide), jnp.float32)], axis=1
            )
            taken = pltpu.roll(taken, (py * q - (SIDE - OV)) % length, 1)
            pieces = taken if pieces is None else pieces + taken
        flat[...] = pieces
        summed = jnp.zeros((vectors, length), jnp.float32)
        for a in range(lines):
            summed = summed + basis[:, a * length:(a + 1) * length] * flat[a:a + 1, :]
        folded = summed[:, :LANES]
        for t in range(1, length // LANES):
            folded = folded + summed[:, t * LANES:(t + 1) * LANES]
        coarse = jnp.sum(folded, axis=1, keepdims=True) * live
        return jnp.sum(jnp.where(spot, coarse, 0.0), axis=0, keepdims=True)

    sublane = lax.broadcasted_iota(jnp.int32, (8, length), 0)

    def weighted(product):
        summed = product[:8]
        for k in range(8, vectors, 8):
            summed = summed + product[k:k + 8]
        return summed

    def eight_sums(pieces):
        for distance in (4, 2, 1):
            low = lax.rem(sublane // distance, 2) == 0
            merged = []
            for one, other in zip(pieces[:distance], pieces[distance:]):
                away = jnp.where(low, other, one)
                back = pltpu.roll(away, distance, 0)
                if distance != 4:
                    back = jnp.where(low, pltpu.roll(away, 8 - distance, 0), back)
                merged.append(jnp.where(low, one, other) + back)
            pieces = merged
        return pieces[0]

    def spread(rows):
        rows = jnp.where(is_coarse, rows, 0.0)
        joined = rows
        for i in range(1, 4):
            joined = joined + pltpu.roll(rows, i, 0)
        summed = jnp.zeros((vectors, LANES), jnp.float32)
        for b in range(devices // 4):
            summed = (
                summed + inverse[:, b * LANES:(b + 1) * LANES] * joined[4 * b + 3:4 * b + 4, :]
            )
        weights = jnp.sum(summed, axis=1, keepdims=True) * live
        weights = jnp.broadcast_to(weights, (vectors, LANES))
        weights = jnp.concatenate([weights] * (length // LANES), axis=1)
        whole = jnp.concatenate(
            [
                eight_sums([
                    weighted(basis[:, a * length:(a + 1) * length] * weights)
                    for a in range(first, first + 8)
                ])
                for first in range(0, lines, 8)
            ],
            axis=0,
        )
        for t in range(wide // LANES):
            total[t] = jnp.zeros((high, LANES), jnp.float32)
        for q in range(group):
            moved = pltpu.roll(whole, (SIDE - OV - py * q) % length, 1)[:, :wide]
            moved = jnp.where(in_patch, moved, 0.0)
            for t in range(wide // LANES):
                total[t, pl.ds(ROWS - OV + q, lines, stride=group), :] = (
                    moved[:, t * LANES:(t + 1) * LANES]
                )
        return get_total()

    def set_total(value):
        for t in range(wide // LANES):
            total[t] = value[:, t * LANES:(t + 1) * LANES]

    def get_total():
        return jnp.concatenate([total[t] for t in range(wide // LANES)], axis=1)

    def around(value):
        rows = value.shape[0]
        return (
            pltpu.roll(value, rows - 1, 0),
            pltpu.roll(value, 1, 0),
            pltpu.roll(value, wide - 1, 1),
            pltpu.roll(value, 1, 1),
        )

    fold_lane = SIDE - OV - 4
    fold_lanes = lax.broadcasted_iota(jnp.int32, (FOLD_ROWS, LANES), 1)
    fold_place = fold_lanes // FOLD
    in_fold = (fold_lanes >= fold_lane) & (fold_lanes < fold_lane + FOLD)

    def folds(di):
        away = [height + i * FOLD_ROWS for i in range(3)]
        near_rows = [i * FOLD_ROWS for i in range(3)]
        return (away, near_rows) if di == 1 else (near_rows, away)

    def exchange(turn, meanwhile=lambda: None):
        start_all(part_copy(turn), directions[turn], corner=False)
        for number, (di, dj) in enumerate(CORNERS):
            side = part[turn, :, wide - LANES:] if dj == 1 else part[turn, :, :LANES]
            folded = jnp.zeros((FOLD_ROWS, LANES), jnp.float32)
            for strip_number, row in enumerate(folds(di)[0]):
                moved = pltpu.roll(
                    side[row:row + FOLD_ROWS], (FOLD * strip_number - fold_lane) % LANES, 1
                )
                folded = jnp.where(fold_place == strip_number, moved, folded)
            corners[turn, number] = folded
        start_all(part_copy(turn), directions[turn], corner=True)
        set_total(part[turn])
        found = meanwhile()
        receive_all(part_copy(turn), directions[turn])
        for number, (di, dj) in enumerate(directions[turn]):
            _, _, rows, columns = part_slices(turn, di, dj, height, breadth)
            got = arrived[turn][number][...]
            first = columns.start // LANES
            if (di, dj) in CORNERS:
                for strip_number, row in enumerate(folds(di)[1]):
                    moved = pltpu.roll(got, (fold_lane - FOLD * strip_number) % LANES, 1)
                    moved = jnp.where(in_fold, moved, 0.0)
                    at = pl.ds(row, FOLD_ROWS)
                    total[first, at, :] = total[first, at, :] + moved
                continue
            for t in range(columns.size // LANES):
                total[first + t, rows, :] = (
                    total[first + t, rows, :] + got[:, t * LANES:(t + 1) * LANES]
                )
        return jnp.where(inside, get_total(), 0.0), found

    def dots(pairs, first=0):
        row = jnp.zeros((1, LANES), jnp.float32)
        place = lax.rem(quarter + 1, 4) * strip
        for i, (one, other) in enumerate(pairs):
            product = jnp.sum(jnp.where(own, one * other, 0.0), axis=0, keepdims=True)
            value = jnp.sum(product, axis=1, keepdims=True)
            row = jnp.where(row_lane == place + first + i, value, row)
        return row

    def whole_sums(rows, count):
        others = jnp.where(is_coarse, 0.0, rows)
        row = jnp.sum(others, axis=0, keepdims=True)
        return [
            jnp.sum(jnp.where(lax.rem(row_lane, strip) == i, row, 0.0), axis=1, keepdims=True)
            for i in range(count)
        ]

    receive_all(source_copy, NEAR)
    first_vector = pltpu.roll(grown[...], wide + LANES - SIDE, 1)[:, :wide]
    set_total(first_vector)
    loads[7].wait()
    row_out[0] = restrict()
    share(0)

    def build(rows):
        count = rows.stop - rows.start
        side_lane = lax.broadcasted_iota(jnp.int32, (count, LANES), 1)
        patch = []
        for f in range(4):
            base = jnp.concatenate(
                [fields[f, rows, :], jnp.zeros((count, LANES), jnp.float32)], axis=1
            )
            base = pltpu.roll(base, SIDE, 1)
            west = pltpu.roll(pack_in[0, rows, :], (SIDE - (f + 1) * strip) % LANES, 1)
            east = pltpu.roll(pack_in[1, rows, :], (SIDE - f * strip) % LANES, 1)
            left = jnp.where(
                (side_lane >= SIDE - strip) & (side_lane < SIDE), west, base[:, :LANES]
            )
            right = jnp.where(
                (side_lane >= SIDE) & (side_lane < SIDE + strip), east, base[:, wide - LANES:]
            )
            patch.append(jnp.concatenate([left, base[:, LANES:wide - LANES], right], axis=1))
        level = jnp.exp(0.5 * patch[0])
        level_inverse = jnp.exp(-0.5 * patch[0])
        root_along, root_across = patch[1], patch[2]
        faces = (
            root_along * pltpu.roll(root_along, count - 1, 0),
            root_along * pltpu.roll(root_along, 1, 0),
            root_across * pltpu.roll(root_across, wide - 1, 1),
            root_across * pltpu.roll(root_across, 1, 1),
        )
        outflow = jnp.zeros((count, wide), jnp.float32)
        for face, beside in zip(faces, around(level_inverse)):
            outflow = outflow + face * beside
        diagonal = patch[3] + level * outflow
        diagonal = jnp.where(diagonal > 0.0, diagonal, 1.0)
        return level, level_inverse, faces, diagonal

    near = slice(ROWS - NARROW, ROWS + height + NARROW)
    middle = slice(NARROW, NARROW + height)
    mine = slice(ROWS, ROWS + height)
    receive_all(field_copy, NEAR)
    level, level_inverse, faces, diagonal = build(near)
    step_size = OMEGA / diagonal
    step_faces = [face * step_size for face in faces]
    step_level = step_size * level
    own_level_inverse = level_inverse[middle]

    def smooth(vector):
        scaled = step_level * vector[near]
        field = scaled
        for sweep in range(SWEEPS - 1):
            moved = (1.0 - OMEGA) * field + scaled
            for face, beside in zip(step_faces, around(field)):
                moved = moved + face * beside
            field = moved
        return jnp.where(own, own_level_inverse * field[middle], 0.0)

    def apply(vector, rows):
        scaled = level[rows] * vector
        image = diagonal[rows] * scaled
        for face, beside in zip(faces, around(scaled)):
            image = image - face[rows] * beside
        return level_inverse[rows] * image

    def put_part(turn, solved, spreads):
        part[turn] = spreads
        part[turn, own_rows, :] = spreads[mine] + solved

    solved = smooth(first_vector)
    receive_all(later_copy, UPRIGHT)
    level, level_inverse, faces, diagonal = build(slice(0, high))
    loads[6].wait()
    put_part(0, solved, spread(collect(0)))
    first_dir, _ = exchange(0)
    image = apply(first_dir, slice(0, high))

    set_total(image)
    first_vector_own, image_own = first_vector[mine], image[mine]
    row_out[1] = restrict() + dots(
        [
            (first_vector_own, first_vector_own),
            (first_vector_own, image_own),
            (image_own, image_own),
        ]
    )
    share(1)
    solved = smooth(image)
    rows = collect(1)
    put_part(1, solved, spread(rows))

    def first_column():
        squares, mixed, image_squares = whole_sums(rows, 3)
        source_norm = jnp.sqrt(squares + EPSILON)
        shrink = 1.0 / source_norm
        first_first = mixed * shrink * shrink
        left_over = (
            image_squares * shrink * shrink
            - 2.0 * first_first * first_first
            + first_first * first_first * (squares * shrink * shrink)
        )
        second_first = jnp.sqrt(jnp.maximum(left_over, 0.0) + EPSILON)
        grow = 1.0 / second_first
        first = first_vector_own * shrink
        second = (image_own * shrink - first_first * first) * grow
        radius_inverse = lax.rsqrt(first_first * first_first + second_first * second_first)
        products = [(first, first), (second, second), (first, second)]
        return (
            source_norm, shrink, first_first, second_first, grow, first, second,
            radius_inverse, first_first * radius_inverse, second_first * radius_inverse,
            first_dir[near] * shrink, dots(products, 3),
        )

    second_dir, found = exchange(1, first_column)
    (
        source_norm, shrink, first_first, second_first, grow, first, second,
        radius_inverse, cosine, sine, first_dir, known_dots,
    ) = found
    second_dir = (second_dir[near] * shrink - first_first * first_dir) * grow
    image = apply(second_dir, near)[middle]
    first_dir, second_dir = first_dir[middle], second_dir[middle]
    row_out[2] = known_dots + dots([(first, image), (second, image), (image, image)])
    share(2)
    sent_all(source_copy, NEAR)
    sent_all(field_copy, NEAR)
    sent_all(later_copy, UPRIGHT)
    for turn in range(2):
        sent_all(part_copy(turn), directions[turn])
        row_bytes(turn, row_send).wait()
    first_second, second_second, image_squares, ones, twos, cross = whole_sums(collect(2), 6)
    left_over = (
        image_squares
        - 2.0 * (first_second * first_second + second_second * second_second)
        + first_second * first_second * ones
        + second_second * second_second * twos
        + 2.0 * first_second * second_second * cross
    )
    third_square = jnp.maximum(left_over, 0.0) + EPSILON
    image = image - first_second * first - second_second * second
    upper_right = cosine * first_second + sine * second_second
    lower_right = cosine * second_second - sine * first_second
    weight_two = (
        lower_right * (-sine * source_norm) / (lower_right * lower_right + third_square)
    )
    weight_one = (cosine * source_norm - upper_right * weight_two) * radius_inverse
    remainder_one = source_norm - first_first * weight_one - first_second * weight_two
    remainder_two = -second_first * weight_one - second_second * weight_two
    answer = weight_one * first_dir + weight_two * second_dir
    remainder = remainder_one * first + remainder_two * second - weight_two * image
    both_out[0] = pltpu.roll(answer, wide - SIDE, 1)[:, :breadth]
    both_out[1] = pltpu.roll(remainder, wide - SIDE, 1)[:, :breadth]
    row_bytes(2, row_send).wait()


def on_device(
    gx, gy,
    source, potential, mobility_along, mobility_across, recombination, counts, basis, coarse_inverse
):
    height, breadth = source.shape
    vectors = basis.shape[0]
    devices = gx * gy
    high, wide = height + 2 * ROWS, breadth + 2 * SIDE
    px, py = height + 2 * OV, breadth + 2 * OV
    group = LANES // math.gcd(py, LANES)
    far = FAR if gx > 2 else []
    arrived = []
    for turn, chosen in enumerate((NEAR + far, NEAR)):
        for di, dj in chosen:
            rows, columns, _, _ = part_slices(turn, di, dj, height, breadth)
            shape = (rows.size, columns.size)
            if (di, dj) in CORNERS:
                shape = (FOLD_ROWS, LANES)
            arrived.append(pltpu.VMEM(shape, jnp.float32))
    vmem = pl.BlockSpec(memory_space=pltpu.VMEM)
    hbm = pl.BlockSpec(memory_space=pltpu.HBM)
    ways = len(NEAR + far)
    both = pl.pallas_call(
        functools.partial(kernel, gx, gy, far),
        out_shape=jax.ShapeDtypeStruct((2, height, breadth), jnp.float32),
        in_specs=[hbm] * 8,
        out_specs=vmem,
        scratch_shapes=[
            pltpu.SMEM((1, 1), jnp.int32),
            pltpu.VMEM(basis.shape, jnp.float32),
            pltpu.VMEM(coarse_inverse.shape, jnp.float32),
            pltpu.VMEM((high, breadth + 2 * LANES), jnp.float32),
            pltpu.VMEM((2, height, breadth), jnp.float32),
            pltpu.VMEM((4, high, breadth), jnp.float32),
            pltpu.VMEM((2, height, LANES), jnp.float32),
            pltpu.VMEM((2, high, LANES), jnp.float32),
            pltpu.VMEM((2, high, wide), jnp.float32),
            pltpu.VMEM((2, len(CORNERS), FOLD_ROWS, LANES), jnp.float32),
            pltpu.VMEM((wide // LANES, high, LANES), jnp.float32),
            pltpu.VMEM((px // group, py * group), jnp.float32),
            pltpu.VMEM((3, 1, LANES), jnp.float32),
            pltpu.VMEM((3, devices, 1, LANES), jnp.float32),
            *arrived,
            pltpu.SemaphoreType.DMA((8,)),
            pltpu.SemaphoreType.DMA((5, ways)),
            pltpu.SemaphoreType.DMA((5, ways)),
            pltpu.SemaphoreType.DMA((3,)),
            pltpu.SemaphoreType.DMA((3,)),
        ],
        compiler_params=pltpu.CompilerParams(
            collective_id=0, has_side_effects=True, vmem_limit_bytes=VMEM_GRANT
        ),
    )(counts, source, potential, mobility_along, mobility_across, recombination, basis, coarse_inverse)
    return both[0], both[1]


def solution(mesh):
    placed = (P("gx", "gy"),) * 7 + (P(("gx", "gy"), None),)
    return jax.shard_map(
        functools.partial(on_device, mesh.shape["gx"], mesh.shape["gy"]),
        mesh=mesh,
        in_specs=placed,
        out_specs=(P("gx", "gy"), P("gx", "gy")),
        check_vma=False,
    )
```
